32 devices in a mesh: dp: 8 (over y, x, core), tensor: 4 (over z).
Axes of the slice: x: 2, y: 2, z: 4, core: 2. Of those that a mesh axis runs over, the one named last changes fastest.
Arguments:
- inputs: bfloat16 [2, 8, 1024, 2048], P(None, 'dp', 'tensor'), may hold values from -8 to 8
- w_query: bfloat16 [1, 2048, 2048], P(None, 'dp', 'tensor'), may hold values from -0.125 to 0.125
- w_key: bfloat16 [1, 2048, 2048], P(None, 'dp', 'tensor'), may hold values from -0.125 to 0.125
- w_value: bfloat16 [1, 2048, 3456], P(None, 'dp', 'tensor'), may hold values from -0.125 to 0.125
- w_gate: bfloat16 [1, 2048, 3456], P(None, 'dp', 'tensor'), may hold values from -0.125 to 0.125
- w_out: bfloat16 [1, 3456, 2048], P(None, 'tensor', 'dp'), may hold values from -0.109375 to 0.109375
- w_act: bfloat16 [1, 2048, 3456], P(None, 'dp', 'tensor'), may hold values from -0.125 to 0.125
- w_lin: bfloat16 [1, 2048, 3456], P(None, 'dp', 'tensor'), may hold values from -0.125 to 0.125
- w_down: bfloat16 [1, 3456, 2048], P(None, 'tensor', 'dp'), may hold values from -0.109375 to 0.109375
- gain_mix: bfloat16 [1, 2048], P(None, 'dp'), may hold values from 0.25 to 1.75
- gain_ffn: bfloat16 [1, 2048], P(None, 'dp'), may hold values from 0.25 to 1.75
- cotangent: bfloat16 [2, 8, 1024, 2048], P(None, 'dp', 'tensor'), may hold values from -8 to 8
Outputs:
- output: bfloat16 [2, 8, 1024, 2048], P(None, 'dp', 'tensor')
- grad_input: float32 [2, 8, 1024, 2048], P(None, 'dp', 'tensor')
- grad_query: float32 [1, 2048, 2048], P(None, 'dp', 'tensor')
- grad_key: float32 [1, 2048, 2048], P(None, 'dp', 'tensor')
- grad_value: float32 [1, 2048, 3456], P(None, 'dp', 'tensor')
- grad_gate: float32 [1, 2048, 3456], P(None, 'dp', 'tensor')
- grad_out: float32 [1, 3456, 2048], P(None, 'tensor', 'dp')
- grad_act: float32 [1, 2048, 3456], P(None, 'dp', 'tensor')
- grad_lin: float32 [1, 2048, 3456], P(None, 'dp', 'tensor')
- grad_down: float32 [1, 3456, 2048], P(None, 'tensor', 'dp')
- grad_gain_mix: float32 [1, 2048], P(None, 'dp')
- grad_gain_ffn: float32 [1, 2048], P(None, 'dp')
The draws below stay inside these ranges and needn't reach their ends.
All inputs are finite; a program needn't handle non-finite values.
Results may differ from the reference program's by a relative error of at most 0.02.
Values may be sent and summed in bfloat16 or wider, within the bound.
No kernel may reach another device: no remote copies, remote signals or barrier semaphores. Data moves between devices by JAX's collectives and lax.ppermute only.
A program may use at most 256 MiB of HBM per device.

```python
import jax
import jax.numpy as jnp
from jax import lax

D = 2048
H = 8
DK = 256
DV = 432
FF = 3456
SEQ = 1024
MB = 2
LAYERS = 1
BATCH = 8


def spiked(array, rng, source, target, blocks, factor):
    def block_of(dim):
        return (jnp.arange(array.shape[dim]) // (array.shape[dim] // blocks)).reshape((-1,) + (1,) * (array.ndim - 1 - dim))

    near = jax.random.permutation(rng, blocks)[block_of(target)]
    other_side = (block_of(target) + blocks // 2) % blocks
    return jnp.where((block_of(source) == near) | (block_of(source) == other_side), factor * array, array)


def shard_levels(key, extent, shards, low, largest):
    gain, own = 1.0, jax.random.fold_in(key, 6)
    for position, blocks in shards:
        steps = jnp.exp(jax.random.uniform(jax.random.fold_in(own, position), (blocks,), jnp.float32, low / len(shards), largest / len(shards)))
        gain = gain * jnp.repeat(steps, extent[position] // blocks).reshape([-1 if axis == position else 1 for axis in range(len(extent))])
    return gain


def noise(rng, extent, scale, limit, split=(), held_as=jnp.bfloat16):
    gain = shard_levels(rng, extent, split, -0.22, 0.18) if split else 1.0
    result = jax.random.normal(rng, extent, jnp.float32) * scale * gain
    return jnp.minimum(jnp.maximum(result, -limit), limit).astype(held_as)


def heavy_noise(rng, extent, deviation, most, cuts, heavy, kind=jnp.bfloat16):
    values = deviation * jax.random.normal(rng, extent, jnp.float32)
    if cuts:
        values = values * shard_levels(rng, extent, cuts, -0.22, 0.18)
    return jnp.clip(spiked(values, jax.random.fold_in(rng, 3), *heavy), -most, most).astype(kind)


def setup_inputs(seed: int = 0) -> dict:
    seeds = jax.random.split(jax.random.key(seed), 13)
    inputs = heavy_noise(seeds[0], (MB, BATCH, SEQ, D), 1.0, 8.0, ((1, 8), (2, 4)), (1, 3, 8, 2.0))
    w_query = noise(seeds[1], (LAYERS, D, H * DK), D ** -0.5, 0.125, ((1, 8), (2, 4)))
    w_key = noise(seeds[2], (LAYERS, D, H * DK), D ** -0.5, 0.125, ((1, 8), (2, 4)))
    w_value = noise(seeds[3], (LAYERS, D, H * DV), D ** -0.5, 0.125, ((1, 8), (2, 4)))
    w_gate = noise(seeds[4], (LAYERS, D, H * DV), D ** -0.5, 0.125, ((1, 8), (2, 4)))
    w_out = noise(seeds[5], (LAYERS, H * DV, D), (H * DV) ** -0.5, 0.109375, ((1, 4), (2, 8)))
    w_act = noise(seeds[6], (LAYERS, D, FF), D ** -0.5, 0.125, ((1, 8), (2, 4)))
    w_lin = noise(seeds[7], (LAYERS, D, FF), D ** -0.5, 0.125, ((1, 8), (2, 4)))
    w_down = noise(seeds[8], (LAYERS, FF, D), FF ** -0.5, 0.109375, ((1, 4), (2, 8)))
    gain_mix = jnp.clip(1.0 + 0.15 * jax.random.normal(seeds[9], (LAYERS, D), jnp.float32), 0.25, 1.75).astype(jnp.bfloat16)
    gain_ffn = jnp.clip(1.0 + 0.15 * jax.random.normal(seeds[10], (LAYERS, D), jnp.float32), 0.25, 1.75).astype(jnp.bfloat16)
    cotangent = heavy_noise(seeds[11], (MB, BATCH, SEQ, D), 1.0, 8.0, ((1, 8), (2, 4)), (1, 3, 8, 2.0))
    return dict(inputs=inputs, w_query=w_query, w_key=w_key, w_value=w_value, w_gate=w_gate, w_out=w_out, w_act=w_act, w_lin=w_lin, w_down=w_down, gain_mix=gain_mix, gain_ffn=gain_ffn, cotangent=cotangent)


eps_norm = 1e-06
group_eps = 1.0

@jax.custom_vjp
def low(v):
    return lax.optimization_barrier(v.astype(jnp.bfloat16)).astype(jnp.float32)

@jax.custom_vjp
def low_back(v):
    return v

def low_keep(v):
    return (low(v), None)

def low_pass(kept, grad):
    return (grad,)

def back_keep(v):
    return (v, None)

def back_low(kept, grad):
    return (low(grad),)
low.defvjp(low_keep, low_pass)
low_back.defvjp(back_keep, back_low)

def decay_table(head_count, first_head, length, key_size):
    head_ids = (first_head + jnp.arange(head_count, dtype=jnp.int32)).astype(jnp.float32)
    log_rates = jnp.log(1.0 - jnp.exp2(-5.0 - head_ids))
    positions = jnp.arange(length, dtype=jnp.int32)
    offsets = (positions[:, None] - positions[None, :]).astype(jnp.float32)
    causal = offsets >= 0.0
    powers = jnp.exp(jnp.where(causal, offsets, 0.0)[None] * log_rates[:, None, None])
    return jnp.where(causal[None], powers, 0.0) * key_size ** (-0.5)

def rms_inverse(stream, eps_value):
    return lax.rsqrt(lax.optimization_barrier(jnp.mean(stream * stream, axis=-1, keepdims=True)) + eps_value)

def one_layer(stream, w_query, w_key, w_value, w_gate, w_out, w_act, w_lin, w_down, gain_mix, gain_ffn):
    highest = lax.Precision.HIGHEST
    length = stream.shape[0]
    normed_in = low(stream * rms_inverse(stream, eps_norm) * gain_mix)
    queries = low_back(low(jnp.dot(normed_in, w_query, precision=highest)))
    key_rows = low_back(low(jnp.dot(normed_in, w_key, precision=highest)))
    values = low_back(low(jnp.dot(normed_in, w_value, precision=highest)))
    gate_pre = low_back(jnp.dot(normed_in, w_gate, precision=highest))
    query_heads = queries.reshape(length, H, DK)
    key_heads = key_rows.reshape(length, H, DK)
    value_heads = values.reshape(length, H, DV)
    scores = low_back(jnp.einsum('nhk,mhk->hnm', query_heads, key_heads, precision=highest))
    weights_mix = low(scores * decay_table(H, 0, length, DK))
    retained = low_back(jnp.einsum('hnm,mhv->nhv', weights_mix, value_heads, precision=highest))
    normed = retained * rms_inverse(retained, group_eps)
    merged = low((jax.nn.silu(gate_pre.reshape(length, H, DV)) * normed).reshape(length, H * DV))
    middle = stream + low_back(jnp.dot(merged, w_out, precision=highest))
    normed_mid = low(middle * rms_inverse(middle, eps_norm) * gain_ffn)
    act_pre = low_back(jnp.dot(normed_mid, w_act, precision=highest))
    lin_pre = low_back(jnp.dot(normed_mid, w_lin, precision=highest))
    hidden = low(jax.nn.gelu(act_pre) * lin_pre)
    return middle + low_back(jnp.dot(hidden, w_down, precision=highest))

def forward_net(stream, params):
    for layer_id in range(params[0].shape[0]):
        stream = one_layer(stream, *[weight_arg[layer_id] for weight_arg in params])
    return stream

def reference(inputs, w_query, w_key, w_value, w_gate, w_out, w_act, w_lin, w_down, gain_mix, gain_ffn, cotangent):
    params = tuple((weight_arg.astype(jnp.float32) for weight_arg in (w_query, w_key, w_value, w_gate, w_out, w_act, w_lin, w_down, gain_mix, gain_ffn)))
    seq_count = inputs.shape[0] * inputs.shape[1]
    flat_in = inputs.astype(jnp.float32).reshape(seq_count, inputs.shape[2], inputs.shape[3])
    flat_cot = cotangent.astype(jnp.float32).reshape(seq_count, inputs.shape[2], inputs.shape[3])

    def seq_step(totals, seq_pair):
        out_seq, pullback = jax.vjp(forward_net, seq_pair[0], params)
        grad_seq, grad_params = pullback(seq_pair[1])
        return (jax.tree.map(jnp.add, totals, grad_params), (out_seq, grad_seq))
    zero_grads = jax.tree.map(jnp.zeros_like, params)
    totals, results = lax.scan(seq_step, zero_grads, (flat_in, flat_cot))
    output = results[0].reshape(inputs.shape).astype(jnp.bfloat16)
    grad_input = results[1].reshape(inputs.shape)
    return (output, grad_input, totals[0], totals[1], totals[2], totals[3], totals[4], totals[5], totals[6], totals[7], totals[8], totals[9])
```

```python
import functools
import jax
import jax.numpy as jnp
from jax import lax
from jax.experimental import pallas as pl
from jax.experimental.pallas import tpu as pltpu
from jax.sharding import PartitionSpec as P

DK = 256
SEQ = 1024


eps_norm = 1e-06
group_eps = 1.0


def decay_table(head_count, first_head, length, key_size):
    head_ids = (first_head + jnp.arange(head_count, dtype=jnp.int32)).astype(jnp.float32)
    log_rates = jnp.log(1.0 - jnp.exp2(-5.0 - head_ids))
    positions = jnp.arange(length, dtype=jnp.int32)
    offsets = (positions[:, None] - positions[None, :]).astype(jnp.float32)
    causal = offsets >= 0.0
    powers = jnp.exp(jnp.where(causal, offsets, 0.0)[None] * log_rates[:, None, None])
    return jnp.where(causal[None], powers, 0.0) * key_size ** (-0.5)


def rms_inverse(stream, eps_value):
    return lax.rsqrt(jnp.mean(stream * stream, axis=-1, keepdims=True) + eps_value)


def spread_rows(normed_rows):
    return lax.all_gather(normed_rows, "tensor", axis=1, tiled=True)


def collect_rows(partial_value):
    return lax.psum_scatter(
        partial_value.astype(jnp.bfloat16), "tensor", scatter_dimension=1, tiled=True
    ).astype(jnp.float32)


def spread_grads(grad_rows):
    return lax.all_gather(grad_rows, "tensor", axis=1, tiled=True)


def collect_grads(partial_value):
    return lax.psum_scatter(
        partial_value.astype(jnp.bfloat16), "tensor", scatter_dimension=1, tiled=True
    ).astype(jnp.float32)


def fetch_layer(weight_set, layer_id):
    return (
        lax.all_gather(weight_set[0][layer_id], "dp", axis=0, tiled=True),
        lax.all_gather(weight_set[1][layer_id], "dp", axis=0, tiled=True),
        lax.all_gather(weight_set[2][layer_id], "dp", axis=0, tiled=True),
        lax.all_gather(weight_set[3][layer_id], "dp", axis=0, tiled=True),
        lax.all_gather(weight_set[4][layer_id], "dp", axis=1, tiled=True),
        lax.all_gather(weight_set[5][layer_id], "dp", axis=0, tiled=True),
        lax.all_gather(weight_set[6][layer_id], "dp", axis=0, tiled=True),
        lax.all_gather(weight_set[7][layer_id], "dp", axis=1, tiled=True),
        lax.all_gather(weight_set[8][layer_id], "dp", axis=0, tiled=True),
        lax.all_gather(weight_set[9][layer_id], "dp", axis=0, tiled=True),
    )


def project(in_rows, weight_mat):
    return jnp.einsum("bsd,de->bse", in_rows, weight_mat, preferred_element_type=jnp.float32)


def project_back(grad_rows, weight_mat):
    return jnp.einsum("bse,de->bsd", grad_rows, weight_mat, preferred_element_type=jnp.float32)


def weight_grad(in_rows, grad_rows):
    return jnp.einsum("bsd,bse->de", in_rows, grad_rows, preferred_element_type=jnp.float32)


def mix_forward(normed_in, layer_w, decays):
    batch_here = normed_in.shape[0]
    length = normed_in.shape[1]
    heads_here = decays.shape[0]
    queries = (
        project(normed_in, layer_w[0])
        .astype(jnp.bfloat16)
        .reshape(batch_here, length, heads_here, -1)
    )
    key_rows = (
        project(normed_in, layer_w[1])
        .astype(jnp.bfloat16)
        .reshape(batch_here, length, heads_here, -1)
    )
    values = (
        project(normed_in, layer_w[2])
        .astype(jnp.bfloat16)
        .reshape(batch_here, length, heads_here, -1)
    )
    gate_pre = project(normed_in, layer_w[3]).reshape(batch_here, length, heads_here, -1)
    scores = jnp.einsum("bnhk,bmhk->bhnm", queries, key_rows, preferred_element_type=jnp.float32)
    weights_mix = (scores * decays[None]).astype(jnp.bfloat16)
    retained = jnp.einsum(
        "bhnm,bmhv->bnhv", weights_mix, values, preferred_element_type=jnp.float32
    )
    inv_scale = rms_inverse(retained, group_eps)
    normed = retained * inv_scale
    merged = (jax.nn.silu(gate_pre) * normed).astype(jnp.bfloat16).reshape(batch_here, length, -1)
    partial_value = project(merged, layer_w[4])
    return (
        partial_value,
        (queries, key_rows, values, gate_pre, weights_mix, inv_scale, normed, merged),
    )


def mix_backward(normed_in, layer_w, decays, kept, grad_rows):
    queries, key_rows, values, gate_pre, weights_mix, inv_scale, normed, merged = kept
    batch_here = normed_in.shape[0]
    length = normed_in.shape[1]
    grad_w_out = weight_grad(merged, grad_rows)
    merged_grad = jnp.einsum(
        "bsd,ed->bse", grad_rows, layer_w[4], preferred_element_type=jnp.float32
    ).reshape(normed.shape)
    swish, swish_back = jax.vjp(jax.nn.silu, gate_pre)
    gate_grad = (
        swish_back(merged_grad * normed)[0].astype(jnp.bfloat16).reshape(batch_here, length, -1)
    )
    normed_grad = merged_grad * swish
    retained_grad = (
        inv_scale * (normed_grad - normed * jnp.mean(normed_grad * normed, axis=-1, keepdims=True))
    ).astype(jnp.bfloat16)
    mix_grad = jnp.einsum(
        "bnhv,bmhv->bhnm", retained_grad, values, preferred_element_type=jnp.float32
    )
    values_grad = (
        jnp.einsum(
            "bhnm,bnhv->bmhv", weights_mix, retained_grad, preferred_element_type=jnp.float32
        )
        .astype(jnp.bfloat16)
        .reshape(batch_here, length, -1)
    )
    score_grad = (mix_grad * decays[None]).astype(jnp.bfloat16)
    queries_grad = (
        jnp.einsum("bhnm,bmhk->bnhk", score_grad, key_rows, preferred_element_type=jnp.float32)
        .astype(jnp.bfloat16)
        .reshape(batch_here, length, -1)
    )
    keys_grad = (
        jnp.einsum("bhnm,bnhk->bmhk", score_grad, queries, preferred_element_type=jnp.float32)
        .astype(jnp.bfloat16)
        .reshape(batch_here, length, -1)
    )
    grads = (
        weight_grad(normed_in, queries_grad),
        weight_grad(normed_in, keys_grad),
        weight_grad(normed_in, values_grad),
        weight_grad(normed_in, gate_grad),
        grad_w_out,
    )
    in_grad = project_back(queries_grad, layer_w[0]) + project_back(keys_grad, layer_w[1])
    in_grad = in_grad + project_back(values_grad, layer_w[2]) + project_back(gate_grad, layer_w[3])
    return (in_grad, grads)


def ffn_forward(normed_mid, layer_w):
    act_pre = project(normed_mid, layer_w[5])
    lin_pre = project(normed_mid, layer_w[6])
    hidden = (jax.nn.gelu(act_pre) * lin_pre).astype(jnp.bfloat16)
    return (project(hidden, layer_w[7]), (act_pre, lin_pre, hidden))


def ffn_backward(normed_mid, layer_w, kept, grad_rows):
    act_pre, lin_pre, hidden = kept
    grad_w_down = weight_grad(hidden, grad_rows)
    grad_hidden = jnp.einsum(
        "bsd,fd->bsf", grad_rows, layer_w[7], preferred_element_type=jnp.float32
    )
    gelu_val, gelu_back = jax.vjp(jax.nn.gelu, act_pre)
    act_grad = gelu_back(grad_hidden * lin_pre)[0].astype(jnp.bfloat16)
    lin_grad = (grad_hidden * gelu_val).astype(jnp.bfloat16)
    in_grad = project_back(act_grad, layer_w[5]) + project_back(lin_grad, layer_w[6])
    return (
        in_grad,
        (weight_grad(normed_mid, act_grad), weight_grad(normed_mid, lin_grad), grad_w_down),
    )


def norm_forward(stream, gain_row):
    return (stream * rms_inverse(stream, eps_norm) * gain_row).astype(jnp.bfloat16)


def norm_backward(stream, gain_row, grad_norm):
    inv_scale = rms_inverse(stream, eps_norm)
    unit_rows = stream * inv_scale
    grad_gain = jnp.sum(grad_norm * unit_rows, axis=(0, 1))
    grad_unit = grad_norm * gain_row
    grad_stream = inv_scale * (
        grad_unit - unit_rows * jnp.mean(grad_unit * unit_rows, axis=-1, keepdims=True)
    )
    return (grad_stream, grad_gain)


def shards(
    inputs,
    w_query,
    w_key,
    w_value,
    w_gate,
    w_out,
    w_act,
    w_lin,
    w_down,
    gain_mix,
    gain_ffn,
    cotangent,
):
    weight_set = (w_query, w_key, w_value, w_gate, w_out, w_act, w_lin, w_down, gain_mix, gain_ffn)
    layer_count = w_query.shape[0]
    micro_count = inputs.shape[0]
    heads_here = w_query.shape[2] // DK
    decays = decay_table(heads_here, lax.axis_index("tensor") * heads_here, SEQ, DK)
    streams = [inputs[micro_id].astype(jnp.float32) for micro_id in range(micro_count)]
    layer_id = 0
    layer_records = []
    for micro_id in range(micro_count):
        current = fetch_layer(weight_set, layer_id)
        stream = streams[micro_id]
        normed_in = spread_rows(norm_forward(stream, current[8].astype(jnp.float32)))
        partial_value, mix_kept = mix_forward(normed_in, current, decays)
        middle = stream + collect_rows(partial_value)
        normed_mid = spread_rows(norm_forward(middle, current[9].astype(jnp.float32)))
        partial_value, ffn_kept = ffn_forward(normed_mid, current)
        streams[micro_id] = middle + collect_rows(partial_value)
        layer_records.append((stream, normed_in, mix_kept, middle, normed_mid, ffn_kept))
    records = [layer_records]
    grads_now = [cotangent[micro_id].astype(jnp.float32) for micro_id in range(micro_count)]
    layer_sums = [None] * layer_count
    for layer_id in reversed(range(layer_count)):
        for micro_id in range(micro_count):
            current = fetch_layer(weight_set, layer_id)
            stream, normed_in, mix_kept, middle, normed_mid, ffn_kept = records[layer_id][micro_id]
            grad_stream = grads_now[micro_id]
            grad_rows = spread_grads(grad_stream.astype(jnp.bfloat16))
            in_grad, ffn_grads = ffn_backward(normed_mid, current, ffn_kept, grad_rows)
            grad_mid, gain_second = norm_backward(
                middle, current[9].astype(jnp.float32), collect_grads(in_grad)
            )
            grad_middle = grad_stream + grad_mid
            grad_rows = spread_grads(grad_middle.astype(jnp.bfloat16))
            in_grad, mix_grads = mix_backward(normed_in, current, decays, mix_kept, grad_rows)
            grad_first, gain_first = norm_backward(
                stream, current[8].astype(jnp.float32), collect_grads(in_grad)
            )
            grads_now[micro_id] = grad_middle + grad_first
            terms = mix_grads + ffn_grads + (gain_first, gain_second)
            if micro_id == 0:
                layer_sums[layer_id] = terms
            else:
                layer_sums[layer_id] = jax.tree.map(jnp.add, layer_sums[layer_id], terms)
    stacked = [jnp.stack([layer_sums[0][kind_id]]) for kind_id in range(10)]
    reduced = (
        lax.psum_scatter(
            stacked[0].astype(jnp.bfloat16), "dp", scatter_dimension=1, tiled=True
        ).astype(jnp.float32),
        lax.psum_scatter(
            stacked[1].astype(jnp.bfloat16), "dp", scatter_dimension=1, tiled=True
        ).astype(jnp.float32),
        lax.psum_scatter(
            stacked[2].astype(jnp.bfloat16), "dp", scatter_dimension=1, tiled=True
        ).astype(jnp.float32),
        lax.psum_scatter(
            stacked[3].astype(jnp.bfloat16), "dp", scatter_dimension=1, tiled=True
        ).astype(jnp.float32),
        lax.psum_scatter(
            stacked[4].astype(jnp.bfloat16), "dp", scatter_dimension=2, tiled=True
        ).astype(jnp.float32),
        lax.psum_scatter(
            stacked[5].astype(jnp.bfloat16), "dp", scatter_dimension=1, tiled=True
        ).astype(jnp.float32),
        lax.psum_scatter(
            stacked[6].astype(jnp.bfloat16), "dp", scatter_dimension=1, tiled=True
        ).astype(jnp.float32),
        lax.psum_scatter(
            stacked[7].astype(jnp.bfloat16), "dp", scatter_dimension=2, tiled=True
        ).astype(jnp.float32),
        lax.psum_scatter(
            stacked[8].astype(jnp.bfloat16), "dp", scatter_dimension=1, tiled=True
        ).astype(jnp.float32),
        lax.psum_scatter(
            stacked[9].astype(jnp.bfloat16), "dp", scatter_dimension=1, tiled=True
        ).astype(jnp.float32),
    )
    gain_sums = lax.psum((reduced[8], reduced[9]), "tensor")
    output = jnp.stack(streams).astype(jnp.bfloat16)
    grad_input = jnp.stack(grads_now)
    return (
        output,
        grad_input,
        reduced[0],
        reduced[1],
        reduced[2],
        reduced[3],
        reduced[4],
        reduced[5],
        reduced[6],
        reduced[7],
        gain_sums[0],
        gain_sums[1],
    )


def cost(flops, bytes_accessed, transcendentals):
    return pl.CostEstimate(int(flops*0.3)+1, 0, int(bytes_accessed*0.3)+1)


F32, BF16 = jnp.float32, jnp.bfloat16


def dot_nt(a, b):
    return lax.dot_general(a, b, (((1,), (1,)), ((), ())), preferred_element_type=F32)


def dot_nn(a, b):
    return lax.dot_general(a, b, (((1,), (0,)), ((), ())), preferred_element_type=F32)


def dot_tn(a, b):
    return lax.dot_general(a, b, (((0,), (0,)), ((), ())), preferred_element_type=F32)


PARAMS = pltpu.CompilerParams(vmem_limit_bytes=48 * 1024 * 1024)
GELU_A = 0.7978845608028654
GELU_B = 0.044715
VM = pl.BlockSpec(memory_space=pltpu.VMEM)
SM = pl.BlockSpec(memory_space=pltpu.SMEM)
ANY = pl.BlockSpec(memory_space=pl.ANY)


def by_case(value, count, body):
    for case in range(count):

        @pl.when(value == case)
        def _(case=case):
            body(case)


def shape_of(shape, dtype):
    return jax.ShapeDtypeStruct(shape, dtype)


def weight_copies(pieces, first, last, held, sems):
    width = pieces[0].shape[1]
    return [
        pltpu.make_async_copy(
            piece.at[pl.ds(first, last - first)], held.at[:, pl.ds(p * width, width)], sems.at[p]
        )
        for p, piece in enumerate(pieces)
    ]


def ffn_kernel(dv, first, x_ref, c_ref, f0, f1, f2, f3, act_ref, held, sems):
    copies = weight_copies((f0, f1, f2, f3), 0, 3 * dv, held, sems)
    for copy in copies:
        copy.start()
    for copy in copies:
        copy.wait()
    act = dot_nt(held[:dv], x_ref[...])
    lin = dot_nt(held[dv : 2 * dv], x_ref[...])
    grad_hidden = dot_nt(held[2 * dv :], c_ref[first : first + x_ref.shape[0]])
    square = act * act
    tanh = jnp.tanh(GELU_A * (act + GELU_B * (square * act)))
    gelu = 0.5 * act * (1.0 + tanh)
    slope = 0.5 * (1.0 + tanh) + 0.5 * act * (1.0 - tanh * tanh) * (
        GELU_A * (1.0 + 3.0 * GELU_B * square)
    )
    act_ref[:dv] = (grad_hidden * lin * slope).astype(BF16)
    act_ref[dv : 2 * dv] = (grad_hidden * gelu).astype(BF16)
    act_ref[2 * dv :] = (gelu * lin).astype(BF16)


def ffn_block(x, cot, pieces, half):
    tokens, dv, width = x.shape[0], pieces[0].shape[0] // 3, pieces[0].shape[1]
    return pl.pallas_call(
        functools.partial(ffn_kernel, dv, half * tokens),
        out_shape=shape_of((3 * dv, tokens), BF16),
        in_specs=[VM, VM] + [ANY] * 4,
        out_specs=VM,
        scratch_shapes=[pltpu.VMEM((3 * dv, 4 * width), BF16), pltpu.SemaphoreType.DMA((4,))],
        compiler_params=PARAMS,
        cost_estimate=cost(
            flops=24 * tokens * dv * width, bytes_accessed=12 << 20, transcendentals=tokens * dv
        ),
        name="ffn_block",
    )(x, cot, *pieces)


def ffn_grad_kernel(dv, x0, x1, c_ref, a0, a1, *outs):
    side = outs[0].shape[1]
    half = x0.shape[0]
    for p, target in enumerate(outs):
        cols = slice(p * side, (p + 1) * side)
        for k in range(3):
            rows = slice(k * dv, (k + 1) * dv)
            parts = (c_ref[:half, cols], c_ref[half:, cols]) if k == 2 else (x0[:, cols], x1[:, cols])
            target[rows] = (dot_nn(a0[rows], parts[0]) + dot_nn(a1[rows], parts[1])).astype(BF16)


def ffn_grad_block(xs, cot, acts):
    rows, side = acts[0].shape[0], cot.shape[1] // 4
    grads = shape_of((rows, side), BF16)
    return pl.pallas_call(
        functools.partial(ffn_grad_kernel, rows // 3),
        out_shape=(grads,) * 4,
        in_specs=[VM] * 5,
        out_specs=(VM,) * 4,
        compiler_params=PARAMS,
        cost_estimate=cost(
            flops=8 * cot.shape[0] * rows * side, bytes_accessed=16 << 20, transcendentals=0
        ),
        name="ffn_grad_block",
    )(*xs, cot, *acts)


def decays(rate, keys, queries):
    down = jnp.exp(-keys.astype(F32) * rate) * 0.0625
    up = jnp.exp(queries.astype(F32) * rate)
    return jnp.where(queries >= keys, down * up, 0.0)


def log_rate(spots_ref):
    return jnp.log(1.0 - jnp.exp2(jnp.full((1, 1), -5.0, F32) - spots_ref[0].astype(F32)))


def tiles_of(x, length):
    half = length // 2
    early = slice(x * half, (x + 1) * half)
    late = slice((1 - x) * half, (2 - x) * half)
    lanes = lax.broadcasted_iota(jnp.int32, (1, half), 1)
    below = lax.broadcasted_iota(jnp.int32, (half, 1), 0)
    every = lax.broadcasted_iota(jnp.int32, (length, 1), 0)
    every = lax.rem(every + x * half, length)
    return (
        (early, early, below, lanes),
        (slice(None), late, every, lanes + half),
    )


def mix_kernel(
    dk, dv, spots_ref, x_ref, m0, m1, m2, m3, vqk_ref, g_ref, nrm_ref, inv_ref, out_ref, held, sems
):
    copies = weight_copies((m0, m1, m2, m3), dv, 3 * dv + 2 * dk, held, sems)
    for copy in copies:
        copy.start()
    for copy in copies:
        copy.wait()
    length = x_ref.shape[0]
    tile = 512

    def step(i, carry):
        rows = pl.ds(pl.multiple_of(i * tile, tile), tile)
        g_ref[:, rows] = dot_nt(held[:dv], x_ref[rows])
        vqk_ref[:, rows] = dot_nt(held[dv:], x_ref[rows]).astype(BF16)
        return carry

    lax.fori_loop(0, length // tile, step, 0)
    rate = log_rate(spots_ref)

    def attend(x):
        for keys, queries, key_spots, query_spots in tiles_of(x, length):
            scores = dot_tn(vqk_ref[dv + dk :, keys], vqk_ref[dv : dv + dk, queries])
            weights = (scores * decays(rate, key_spots, query_spots)).astype(BF16)
            retained = dot_nn(vqk_ref[:dv, keys], weights)
            inv = lax.rsqrt(jnp.mean(retained * retained, axis=0, keepdims=True) + 1.0)
            nrm = retained * inv
            gate = g_ref[:, queries]
            nrm_ref[:, queries] = nrm
            inv_ref[:, queries] = inv
            out_ref[:, queries] = (gate / (1.0 + jnp.exp(-gate)) * nrm).astype(BF16)

    by_case(spots_ref[1], 2, attend)


def mix_block(spots, x, pieces, dk, dv):
    tokens, width = x.shape[0], pieces[0].shape[1]
    return pl.pallas_call(
        functools.partial(mix_kernel, dk, dv),
        out_shape=(
            shape_of((dv + 2 * dk, tokens), BF16),
            shape_of((dv, tokens), F32),
            shape_of((dv, tokens), F32),
            shape_of((1, tokens), F32),
            shape_of((dv, tokens), BF16),
        ),
        in_specs=[SM, VM] + [ANY] * 4,
        out_specs=(VM,) * 5,
        scratch_shapes=[
            pltpu.VMEM((2 * dv + 2 * dk, 4 * width), BF16),
            pltpu.SemaphoreType.DMA((4,)),
        ],
        compiler_params=PARAMS,
        cost_estimate=cost(
            flops=2 * tokens * (2 * dk + 2 * dv) * x.shape[1] + 2 * tokens * tokens * (dk + dv),
            bytes_accessed=17 << 20,
            transcendentals=tokens * dv,
        ),
        name="mix_block",
    )(spots, x, *pieces)


def mix_back_kernel(
    dk, dv, spots_ref, s0, s1, m0, m1, m2, m3, vqk_ref, g_ref, nrm_ref, inv_ref,
    grad_ref, held, dv_ref, dk_ref, rg_ref, sems
):
    copies = weight_copies((m0, m1, m2, m3), 0, dv, held, sems)
    for copy in copies:
        copy.start()
    for copy in copies:
        copy.wait()
    half = s0.shape[0]
    length = 2 * half
    q_rows, k_rows = slice(2 * dv, 2 * dv + dk), slice(2 * dv + dk, 2 * dv + 2 * dk)
    for i, s_ref in enumerate((s0, s1)):
        rows = slice(i * half, (i + 1) * half)
        merged_grad = dot_nt(held[...], s_ref[...])
        gate, nrm = g_ref[:, rows], nrm_ref[:, rows]
        sig = 1.0 / (1.0 + jnp.exp(-gate))
        grad_ref[:dv, rows] = (merged_grad * nrm * (sig * (1.0 + gate * (1.0 - sig)))).astype(BF16)
        normed_grad = merged_grad * (gate * sig)
        mean = jnp.mean(normed_grad * nrm, axis=0, keepdims=True)
        rg_ref[:, rows] = (inv_ref[:, rows] * (normed_grad - nrm * mean)).astype(BF16)
    rate = log_rate(spots_ref)
    def attend(x):
        early, late = tiles_of(x, length)
        for keys, queries, key_spots, query_spots in (late, early):
            decay = decays(rate, key_spots, query_spots)
            k_part, q_part = vqk_ref[dv + dk :, keys], vqk_ref[dv : dv + dk, queries]
            rg_part = rg_ref[:, queries]
            weights = (dot_tn(k_part, q_part) * decay).astype(BF16)
            score_grad = (dot_tn(vqk_ref[:dv, keys], rg_part) * decay).astype(BF16)
            grad_ref[q_rows, queries] = dot_nn(k_part, score_grad).astype(BF16)
            values_grad = dot_nt(rg_part, weights)
            keys_grad = dot_nt(q_part, score_grad)
            if keys == slice(None):
                dv_ref[...] = values_grad
                dk_ref[...] = keys_grad
            else:
                dv_ref[:, keys] += values_grad
                dk_ref[:, keys] += keys_grad

    by_case(spots_ref[1], 2, attend)
    grad_ref[dv : 2 * dv] = dv_ref[...].astype(BF16)
    grad_ref[k_rows] = dk_ref[...].astype(BF16)


def mix_back_block(spots, sides, pieces, kept, dk, dv):
    tokens, width = 2 * sides[0].shape[0], pieces[0].shape[1]
    return pl.pallas_call(
        functools.partial(mix_back_kernel, dk, dv),
        out_shape=shape_of((2 * dv + 2 * dk, tokens), BF16),
        in_specs=[SM, VM, VM] + [ANY] * 4 + [VM] * 4,
        out_specs=VM,
        scratch_shapes=[
            pltpu.VMEM((dv, 4 * width), BF16),
            pltpu.VMEM((dv, tokens), F32),
            pltpu.VMEM((dk, tokens), F32),
            pltpu.VMEM((dv, tokens), BF16),
            pltpu.SemaphoreType.DMA((4,)),
        ],
        compiler_params=PARAMS,
        cost_estimate=cost(
            flops=8 * tokens * dv * width + 2 * tokens * tokens * (2 * dv + 3 * dk),
            bytes_accessed=16 << 20,
            transcendentals=tokens * dv,
        ),
        name="mix_back_block",
    )(spots, *sides, *pieces, *kept)


def mix_grad_kernel(dv, s0, s1, x_ref, out_ref, grad_ref, *outs):
    side = outs[0].shape[1]
    count, half = grad_ref.shape[0], s0.shape[0]
    for p, target in enumerate(outs):
        cols = slice(p * side, (p + 1) * side)
        target[:dv] = (
            dot_nn(out_ref[:, :half], s0[:, cols]) + dot_nn(out_ref[:, half:], s1[:, cols])
        ).astype(BF16)
        for rows in (slice(0, dv), slice(dv, 2 * dv), slice(2 * dv, count)):
            target[dv + rows.start : dv + rows.stop] = dot_nn(
                grad_ref[rows], x_ref[:, cols]
            ).astype(BF16)


def mix_grad_block(sides, x, merged, grads):
    dv, side = merged.shape[0], x.shape[1] // 4
    rows = dv + grads.shape[0]
    out = shape_of((rows, side), BF16)
    return pl.pallas_call(
        functools.partial(mix_grad_kernel, dv),
        out_shape=(out,) * 4,
        in_specs=[VM] * 5,
        out_specs=(VM,) * 4,
        compiler_params=PARAMS,
        cost_estimate=cost(
            flops=8 * x.shape[0] * rows * side, bytes_accessed=20 << 20, transcendentals=0
        ),
        name="mix_grad_block",
    )(*sides, x, merged, grads)


def sum_kernel(n_blocks, source_first, first, count, lanes, *refs):
    sources, pieces = refs[:n_blocks], refs[n_blocks : 5 * n_blocks]
    out_ref, held_source, held, source_sems, sems = refs[5 * n_blocks :]
    width = held.shape[2]

    def into(j):
        return pl.ds(j * count, count)

    early = [
        pltpu.make_async_copy(
            sources[j].at[pl.ds(source_first, count), lanes], held_source.at[into(j)], source_sems.at[j]
        )
        for j in range(n_blocks)
    ]
    copies = [
        [
            pltpu.make_async_copy(
                pieces[4 * j + p].at[pl.ds(first, count)], held.at[p, into(j)], sems.at[p, j]
            )
            for j in range(n_blocks)
        ]
        for p in range(4)
    ]
    for copy in early + [copy for group in copies for copy in group]:
        copy.start()
    for copy in early:
        copy.wait()
    for p in range(4):
        for copy in copies[p]:
            copy.wait()
        out_ref[:, p * width : (p + 1) * width] = dot_tn(held_source[...], held[p]).astype(
            out_ref.dtype
        )


def sum_blocks(sources, blocks, source_first, first, count, half, out_type):
    tokens, width, n = sources[0].shape[1], blocks[0][0].shape[1], len(blocks)
    if half is None:
        half = 0
    else:
        tokens = tokens // 2
    return pl.pallas_call(
        functools.partial(
            sum_kernel, n, source_first, first, count, pl.ds(half * tokens, tokens)
        ),
        out_shape=shape_of((tokens, 4 * width), out_type),
        in_specs=[ANY] * (5 * n),
        out_specs=VM,
        scratch_shapes=[
            pltpu.VMEM((n * count, tokens), BF16),
            pltpu.VMEM((4, n * count, width), BF16),
            pltpu.SemaphoreType.DMA((n,)),
            pltpu.SemaphoreType.DMA((4, n)),
        ],
        compiler_params=PARAMS,
        cost_estimate=cost(
            flops=8 * tokens * count * n * width,
            bytes_accessed=8 * count * n * width + 2 * count * n * tokens + 16 * tokens * width,
            transcendentals=0,
        ),
        name="sum_blocks",
    )(*sources, *[piece for block in blocks for piece in block])


def piece_of(p, y, c):
    return 4 * ((p // 2 % 2) ^ y) + 2 * (p % 2) + ((p // 4) ^ c)


def spots_of(x, y, c, z):
    return jnp.stack([x, y, c, z]).astype(jnp.int32)


def split_kernel(at, local, *outs):
    z = at[3]
    width = local.shape[2] // 8

    def split(case):
        for k, out in enumerate(outs):
            micro = lax.rem(z - k + 4, 4) // 2
            for p in range(8):
                first = piece_of(p, case // 2, case % 2) * width
                out[:, p * width : (p + 1) * width] = local[micro, :, first : first + width]

    by_case(2 * at[1] + at[2], 4, split)


def split_blocks(at, local):
    block = shape_of(local.shape[1:], local.dtype)
    return pl.pallas_call(
        split_kernel,
        out_shape=(block,) * 4,
        in_specs=[SM, VM],
        out_specs=(VM,) * 4,
        compiler_params=PARAMS,
        cost_estimate=cost(flops=1196000000, bytes_accessed=3 * local.size * 2, transcendentals=0),
        name="split_blocks",
    )(at, local)


EPS = 1e-6


def assemble_kernel(normed, at, *refs):
    blocks, others = refs[:4], refs[4:8]
    x, c, z = at[0], at[2], at[3]
    here = ((z ^ c) & 1) == x
    count = blocks[0].shape[0]

    def put(sources):
        for k, source in enumerate(sources):
            spot = lax.rem(z + k - 2 * x + 4, 4)
            rows = pl.ds(pl.multiple_of(spot * count, count), count)
            if normed:
                gains, own, out = refs[8:]
                values = source[...].astype(F32)
                scale = lax.rsqrt(jnp.mean(values * values, axis=-1, keepdims=True) + EPS)
                out[rows] = (values * scale * gains[0:1]).astype(BF16)

                @pl.when(spot < 2)
                def _():
                    own[pl.ds(pl.multiple_of(lax.rem(spot, 2) * count, count), count)] = source[...]

            else:
                refs[8][rows] = source[...]

    @pl.when(here)
    def _():
        put(blocks)

    @pl.when(jnp.logical_not(here))
    def _():
        put(others)


def assemble(at, blocks, others, gains=None):
    count, width = blocks[0].shape
    whole, half = shape_of((4 * count, width), BF16), shape_of((2 * count, width), BF16)
    extra = [] if gains is None else [gains]
    return pl.pallas_call(
        functools.partial(assemble_kernel, gains is not None),
        out_shape=whole if gains is None else (half, whole),
        in_specs=[SM] + [VM] * (8 + len(extra)),
        out_specs=VM if gains is None else (VM, VM),
        compiler_params=PARAMS,
        cost_estimate=cost(
            flops=3380000000, bytes_accessed=24 * count * width, transcendentals=0
        ),
        name="assemble",
    )(at, *blocks, *others, *extra)


def middle_kernel(stream, partial, got, gains, middle, normed):
    tile = 128

    def step(i, carry):
        rows = pl.ds(pl.multiple_of(i * tile, tile), tile)
        values = stream[rows].astype(F32) + partial[rows] + got[rows].astype(F32)
        middle[rows] = values
        scale = lax.rsqrt(jnp.mean(values * values, axis=-1, keepdims=True) + EPS)
        normed[rows] = (values * scale * gains[1:2]).astype(BF16)
        return carry

    lax.fori_loop(0, stream.shape[0] // tile, step, 0)


def middle_block(stream, partial, got, gains):
    return pl.pallas_call(
        middle_kernel,
        out_shape=(shape_of(stream.shape, F32), shape_of(stream.shape, BF16)),
        in_specs=[VM] * 4,
        out_specs=(VM, VM),
        compiler_params=PARAMS,
        cost_estimate=cost(flops=3796000000, bytes_accessed=14 * stream.size, transcendentals=0),
        name="middle_block",
    )(stream, partial, got, gains)


def norm_back_kernel(row, base, partial, got, grad, gains, *outs):
    tile = 128
    total_ref = outs[0]
    total_ref[...] = jnp.zeros_like(total_ref)
    gain = gains[row : row + 1]

    def step(i, carry):
        rows = pl.ds(pl.multiple_of(i * tile, tile), tile)
        values = base[rows].astype(F32)
        grad_norm = partial[rows] + got[rows].astype(F32)
        scale = lax.rsqrt(jnp.mean(values * values, axis=-1, keepdims=True) + EPS)
        unit = values * scale
        total_ref[...] += jnp.sum(grad_norm * unit, axis=0, keepdims=True)
        inner = grad_norm * gain
        mean = jnp.mean(inner * unit, axis=-1, keepdims=True)
        result = grad[rows].astype(F32) + scale * (inner - unit * mean)
        for out in outs[1:]:
            out[rows] = result.astype(out.dtype)
        return carry

    lax.fori_loop(0, base.shape[0] // tile, step, 0)


def norm_back_block(row, base, partial, got, grad, gains, types):
    return pl.pallas_call(
        functools.partial(norm_back_kernel, row),
        out_shape=(shape_of((1, base.shape[1]), F32),)
        + tuple(shape_of(base.shape, kind) for kind in types),
        in_specs=[VM] * 5,
        out_specs=(VM,) * (1 + len(types)),
        compiler_params=PARAMS,
        cost_estimate=cost(flops=5200000000, bytes_accessed=20 * base.size, transcendentals=0),
        name="norm_back_block",
    )(base, partial, got, grad, gains)


def spread_kernel(at, own, *refs):
    x, z = at[0], at[3]
    count = refs[0].shape[0]
    for k, out in enumerate(refs[2:]):
        block = lax.rem(z + k, 4)
        rows = pl.ds(pl.multiple_of(lax.rem(block, 2) * count, count), count)

        @pl.when(block // 2 == x)
        def _(out=out, rows=rows):
            out[...] = own[rows]

        for part in range(2):

            @pl.when((block // 2 != x) & (lax.rem(block, 2) == part))
            def _(out=out, other=refs[part]):
                out[...] = other[...]


def spread_blocks(at, own, others):
    block = shape_of((own.shape[0] // 2, own.shape[1]), own.dtype)
    return pl.pallas_call(
        spread_kernel,
        out_shape=(block,) * 4,
        in_specs=[SM, VM, VM, VM],
        out_specs=(VM,) * 4,
        compiler_params=PARAMS,
        cost_estimate=cost(flops=1820000000, bytes_accessed=8 * own.size, transcendentals=0),
        name="spread_blocks",
    )(at, own, *others)


def finish_kernel(at, b0, b1, b2, b3, out):
    x, y, c, z = (at[i] for i in range(4))
    width = out.shape[2] // 8
    for micro in range(2):
        source = lax.rem(z - 2 * micro - (x ^ c) + 8, 4)
        for k, block in enumerate((b0, b1, b2, b3)):

            @pl.when(source == k)
            def _(block=block, micro=micro):
                def put(case):
                    for p in range(8):
                        first = piece_of(p, case // 2, case % 2) * width
                        out[micro, :, first : first + width] = block[
                            :, p * width : (p + 1) * width
                        ].astype(out.dtype)

                by_case(2 * y + c, 4, put)


def finish_tokens(at, blocks, kind):
    count, width = blocks[0].shape
    return pl.pallas_call(
        finish_kernel,
        out_shape=shape_of((2, count, width), kind),
        in_specs=[SM] + [VM] * 4,
        out_specs=VM,
        compiler_params=PARAMS,
        cost_estimate=cost(flops=1560000000, bytes_accessed=16 * count * width, transcendentals=0),
        name="finish_tokens",
    )(at, *blocks)


def rows_kernel(spans, turned, at, mine, got, *refs):
    outs, held = refs[: len(spans)], refs[len(spans)]

    def put(x):
        for out, (first, count), turn in zip(outs, spans, turned):
            target = held if turn else out
            rows = slice(first, first + count)
            target[x * count : (x + 1) * count] = mine[rows].astype(F32)
            target[(1 - x) * count : (2 - x) * count] = got[rows].astype(F32)
            if turn:
                out[...] = held[...].T

    by_case(at[0], 2, put)


def finish_rows(at, mine, got, spans, turned):
    width = mine.shape[1]
    shapes = [(2 * n, width) for _, n in spans]
    held = max([n for (_, n), turn in zip(spans, turned) if turn] + [8])
    return pl.pallas_call(
        functools.partial(rows_kernel, spans, turned),
        out_shape=tuple(
            shape_of(s[::-1] if turn else s, F32) for s, turn in zip(shapes, turned)
        ),
        in_specs=[SM, VM, VM],
        out_specs=(VM,) * len(spans),
        scratch_shapes=[pltpu.VMEM((2 * held, width), F32)],
        compiler_params=PARAMS,
        cost_estimate=cost(flops=1560000000, bytes_accessed=12 * mine.size, transcendentals=0),
        name="finish_rows",
    )(at, mine, got)


O = {'xd': 2, 'yd': 1, 'zd': 2, 'scale': 0.3, 'back': ['B1', 'h3', 'r1', 'u2', 'B2', '|', 'r0', 'x1', 'v1', 'H0', 'x3', 'x2', 'u3', 'B3', 'A', '|', '|', 'Q0', 'v2', 'H1', 'D', '|', 'v3', 'H2', 'L', 'U0', 'U1', 'W', 'e0', 'e1', 'H3', 'f1', 'f0', 'U2', '|', 'f2', 'U3', 'f3', 's', '|', 'Q1', 'e2', 'g1', 't1', 'e3', 'g2', 'm', '|', 't2', 'c1', 'p1', 'c2', 'p2', 'n', 'g3', 't3', 'g0', 't0', 'o', 'c3', '|', '|', 'Q2', 'w', 'p3', 'a1', 'b1', 'T1', 'X', 'c0', 'a2', 'p0', 'b2', 'T2', '|', 'C1', 'Z2', 'a3', 'a0', 'b3', 'T3', '|', 'C2', 'P1', 'P2', 'i', 'b0', 'T0', '|', 'C3', 'P3', 'Q3', 'j', 'k', 'C0', '|', '|', 'G2', 'E0', 'P0', 'M', 'F', 'E1']}


SWAP = ((0, 1), (1, 0))
RING = ((0, 1), (1, 2), (2, 3), (3, 0))
XCZ = ("x", "c", "z")
ORDER = (1, 2, 3, 0)


def prepare_kernel(dk, dv, x_ref, q, k, v, g, o, a, n, d, gains, m_own, m_send, f_own, f_send, turned):
    def put(x, source, own, send, first, count):
        own[first : first + count] = source[x * count : (x + 1) * count]
        send[first : first + count] = source[(1 - x) * count : (2 - x) * count]

    def put_all(x):
        put(x, o, m_own, m_send, 0, dv)
        put(x, g, m_own, m_send, dv, dv)
        put(x, v, m_own, m_send, 2 * dv, dv)
        for i, source in enumerate((q, k)):
            turned[...] = source[...].T
            put(x, turned, m_own, m_send, 3 * dv + i * dk, dk)
        put(x, a, f_own, f_send, 0, dv)
        put(x, n, f_own, f_send, dv, dv)
        put(x, d, f_own, f_send, 2 * dv, dv)

    by_case(x_ref[0], 2, put_all)
    m_own[3 * dv + 2 * dk :] = gains[...]
    m_send[3 * dv + 2 * dk :] = gains[...]


def prepare(at, weights, gains, dk, dv):
    width = gains.shape[1]
    mix = shape_of((3 * dv + 2 * dk + 16, width), BF16)
    ffn = shape_of((3 * dv, width), BF16)
    return pl.pallas_call(
        functools.partial(prepare_kernel, dk, dv),
        out_shape=(mix, mix, ffn, ffn),
        in_specs=[SM] + [VM] * 9,
        out_specs=(VM,) * 4,
        scratch_shapes=[pltpu.VMEM((2 * dk, width), BF16)],
        compiler_params=PARAMS,
        name="prepare",
    )(at, *weights, gains)


def join_kernel(at, own, got, out):
    width = own.shape[1]

    def put(x):
        out[:, x * width : (x + 1) * width] = own[...]
        out[:, (1 - x) * width : (2 - x) * width] = got[...]

    by_case(at[0], 2, put)


def join(at, own, got):
    return pl.pallas_call(
        join_kernel,
        out_shape=shape_of((own.shape[0], 2 * own.shape[1]), BF16),
        in_specs=[SM, VM, VM],
        out_specs=VM,
        compiler_params=PARAMS,
        name="join",
    )(at, own, got)


def tie(value, *others):
    return lax.optimization_barrier((value,) + others)[0]


class Fence:
    def __init__(self):
        self.before, self.now = (), []

    def close(self, *more):
        self.before, self.now = tuple(self.now) + more, []


class Link:
    def __init__(self, fence, depth=1):
        self.fence, self.depth, self.ended = fence, depth, []

    def group(self, sends, *after, fenced=True):
        wait = self.ended[-self.depth] if len(self.ended) >= self.depth else ()
        if fenced:
            wait = wait + self.fence.before
        results = []
        for array, axis, pairs in sends:
            if wait + after:
                array = tie(array, *wait, *after)
            results.append(lax.ppermute(array, axis, pairs))
        self.ended.append(tuple(results))
        if fenced:
            self.fence.now += results
        return results

    def send(self, array, axis, pairs, *after):
        return self.group([(array, axis, pairs)], *after)[0]

    def swap(self, array, axis, *after):
        return self.send(array, axis, SWAP, *after)


def add(*terms):
    total = terms[0].astype(F32)
    for term in terms[1:]:
        total = total + term.astype(F32)
    return total.astype(BF16)


def pick(pair, index):
    return jnp.where(index == 0, pair[0], pair[1])


def home_pairs():
    pairs = []
    for c in range(2):
        for z in range(4):
            home = (z ^ c) & 1
            pairs.append((home * 8 + c * 4 + z, (1 - home) * 8 + c * 4 + z))
    return pairs


def round_pairs(shift):
    pairs = []
    for x in range(2):
        for c in range(2):
            for z in range(4):
                if (z & 1) == (x ^ c):
                    pairs.append((x * 8 + c * 4 + (z + shift) % 4, x * 8 + c * 4 + z))
    return pairs


def turned_pairs(pairs):
    return [(b, a) for a, b in pairs]


def paired(
    inputs,
    w_query,
    w_key,
    w_value,
    w_gate,
    w_out,
    w_act,
    w_lin,
    w_down,
    gain_mix,
    gain_ffn,
    cotangent,
):
    y, x, c, z = (lax.axis_index(name) for name in ("y", "x", "c", "z"))
    at = spots_of(x, y, c, z)
    dk, dv = DK, w_value.shape[2] // 2
    fence = Fence()
    link_x, link_y, link_z = (Link(fence, O[k]) for k in ("xd", "yd", "zd"))
    gains_here = jnp.concatenate(
        [gain_mix, gain_ffn, jnp.zeros((14, gain_mix.shape[1]), gain_mix.dtype)]
    )
    weights = [w_query[0], w_key[0], w_value[0].T, w_gate[0].T, w_out[0]]
    weights += [w_act[0].T, w_lin[0].T, w_down[0]]
    mix_rows, ffn_rows, merged, kept = [None] * 4, [None] * 4, [None] * 4, [None] * 4

    def swap_cores(array):
        return lax.ppermute(array, "c", SWAP)

    def turn_pieces(j, rows, current, over_y):
        rows[j] = (current, over_y) + tuple(
            swap_cores(tie(piece, *fence.before)) for piece in (current, over_y)
        )

    def home_send(block):
        return link_x.send(block, XCZ, home_pairs())

    spots = [jnp.stack([2 * ((z - j) % 4) + x, x]).astype(jnp.int32) for j in range(4)]

    def mix_forward(j, *after):
        kept[j] = mix_block(tie(spots[j], *after, *fence.before), normed_in, mix_rows[j], dk, dv)
        merged[j] = kept[j][-1]
        return merged[j]

    seq_parts = split_blocks(at, inputs[:, 0])
    seq_1, seq_3 = link_z.group([(seq_parts[k], XCZ, round_pairs(k)) for k in (1, 3)])
    mix_own, mix_send, ffn_own, ffn_send = prepare(
        tie(at, seq_parts[0]), weights, gains_here, dk, dv
    )
    mix_start = join(at, mix_own, link_x.swap(mix_send, "x"))
    fence.close()
    first = tie(mix_start, *fence.before)
    over_y = link_y.swap(first, "y")
    mix_1 = link_z.send(first, "z", RING)
    ffn_start = join(at, ffn_own, link_x.swap(ffn_send, "x"))
    other_0 = home_send(seq_parts[0])
    fence.close()
    turn_pieces(0, mix_rows, first, over_y)
    over_y = link_y.swap(ffn_start, "y")
    seq_2 = link_z.send(seq_parts[2], XCZ, round_pairs(2))
    other_1 = home_send(seq_1)
    fence.close()
    cot_parts = split_blocks(tie(at, *fence.before), cotangent[:, 0])
    turn_pieces(0, ffn_rows, ffn_start, over_y)
    over_y = link_y.swap(mix_1, "y")
    mix_2 = link_z.send(mix_1, "z", RING)
    other_3, other_2 = home_send(seq_3), home_send(seq_2)
    gains = jnp.concatenate(
        [piece[3 * dv + 2 * dk :] for piece in mix_rows[0]], axis=1
    ).astype(F32)
    fence.close()
    turn_pieces(1, mix_rows, mix_1, over_y)
    over_y = link_y.swap(mix_2, "y")
    mix_3 = link_z.send(mix_2, "z", RING)
    cot_other = home_send(cot_parts[0])
    own_stream, normed_in = assemble(
        tie(at, *fence.before),
        (seq_parts[0], seq_1, seq_2, seq_3),
        (other_0, other_1, other_2, other_3),
        gains,
    )
    half = own_stream.shape[0]
    fence.now.append(mix_forward(0))
    fence.close()
    mix_blocks = {0: mix_start, 1: mix_1, 2: mix_2, 3: mix_3}
    ffn_blocks = {0: ffn_start}
    mix_over, ffn_over = {2: over_y}, {}
    cot_blocks, cot_others = {0: cot_parts[0]}, {0: cot_other}
    acts, ffn_grads = [[None] * 4, [None] * 4], [None] * 4

    def ffn_sum(first, count, which, kind, *after):
        sources = list(acts[which])
        if after:
            sources[0] = tie(sources[0], *after)
        return sum_blocks(sources, ffn_rows, first, first, count, None, kind)

    class Scatter:
        def __init__(self, blocks):
            self.blocks, self.got, self.ready, self.over, self.running = blocks, {}, {}, {}, None
            self.passed, self.steps = {}, list(ORDER)

        def turn(self, j):
            own_0, own_1, send_0, send_1 = self.blocks[j]
            self.ready[j] = add(own_1, swap_cores(send_1))
            self.got[j] = (own_0, swap_cores(send_0))

        def cross(self, j, *after):
            self.over[j] = link_y.swap(self.ready[j], "y", self.got[j][1], *after)

        def pass_on(self, j):
            assert self.steps.pop(0) == j
            terms = self.got[j] + (self.over[j],)
            if self.running is None:
                self.running = add(*terms)
            else:
                self.passed[j] = link_z.send(self.running, "z", RING)
                self.running = add(self.passed[j], *terms)

    fs = Scatter(ffn_grads)
    V = {}

    def give_back_x(own_half):
        parts = own_half.reshape(2, own_half.shape[0] // 2, -1)
        return link_x.group([(part, XCZ, turned_pairs(home_pairs())) for part in (parts[0], parts[1])])

    def final_swap(block):
        side = block.shape[1] // 2
        keep = pick((block[:, :side], block[:, side:]), x)
        send = pick((block[:, side:], block[:, :side]), x)
        return keep, link_x.swap(send, "x")

    def gain_totals(*sums):
        sums, width = jnp.concatenate(sums), gain_mix.shape[1]
        total = jnp.concatenate(
            [
                lax.dynamic_slice_in_dim(sums, width * lax.bitwise_xor(4 * c + 2 * y, p), width, axis=1)
                for p in (0, 4, 1, 5, 2, 6, 3, 7)
            ],
            axis=1,
        )
        for axis in ("c", "y", "x"):
            total = total + lax.ppermute(tie(total, *fence.before), axis, SWAP)
        fence.now.append(total)
        return total

    def gain_end(total):
        total, width = tie(total, *fence.before), gain_mix.shape[1]
        turned = [
            lax.ppermute(total, "z", [(i, (i + shift) % 4) for i in range(4)]) for shift in (1, 2, 3)
        ]
        fence.now += turned
        total = total + turned[0] + turned[1] + turned[2]
        return lax.dynamic_slice_in_dim(total, width * (4 * y + 2 * x + c), width, axis=1)

    count = 2 * dv + 2 * dk
    token_grads, mix_grads = [None] * 4, [None] * 4
    ms = Scatter(mix_grads)
    last = []
    for step in O["back"]:
        op, j = step[0], int(step[1:] or 0)
        after = tuple(last) + fence.before
        ran = None
        if op == "|":
            fence.close()
        elif op == "h":
            mix_over[j] = link_y.swap(mix_blocks[j], "y")
        elif op == "H":
            ffn_over[j] = link_y.swap(ffn_blocks[j], "y")
        elif op == "u":
            turn_pieces(j, mix_rows, mix_blocks[j], mix_over[j])
        elif op == "U":
            turn_pieces(j, ffn_rows, ffn_blocks[j], ffn_over[j])
        elif op == "v":
            ffn_blocks[j] = link_z.send(ffn_blocks[j - 1], "z", RING)
        elif op == "r":
            shifts = ((2,), (1, 3), (1, 2, 3))[j]
            sends = [(cot_parts[k], XCZ, round_pairs(k)) for k in shifts]
            cot_blocks.update(zip(shifts, link_z.group(sends)))
        elif op == "x":
            cot_others[j] = home_send(cot_blocks[j])
        elif op == "B":
            ran = mix_forward(j, *last)
        elif op == "A":
            ran = V["A"] = sum_blocks([tie(merged[0], *after)] + merged[1:], mix_rows, 0, 0, dv, 1, BF16)
        elif op == "D":
            ran = sum_blocks([tie(merged[0], *after)] + merged[1:], mix_rows, 0, 0, dv, 0, F32)
            V["D"] = ran
        elif op == "L":
            middle, mid_own = middle_block(own_stream, tie(V["D"], *after), V["A"], gains)
            ran = mid_own
            mid_sides = (mid_own, link_x.swap(mid_own, "x"))
        elif op == "W":
            order = range(4)
            cot = assemble(
                tie(at, *after), [cot_blocks[k] for k in order], [cot_others[k] for k in order]
            )
            ran = cot
        elif op in "ef":
            which = "ef".index(op)
            acts[which][j] = ffn_block(tie(mid_sides[which], *after), cot, ffn_rows[j], which)
            ran = acts[which][j]
        elif op == "s":
            ran = V["S"] = ffn_sum(0, 2 * dv, 1, BF16, *after)
        elif op == "g":
            ffn_grads[j] = ffn_grad_block(mid_sides, cot, (tie(acts[0][j], *after), acts[1][j]))
            ran = ffn_grads[j][3]
        elif op == "m":
            ran = ffn_sum(0, 2 * dv, 0, F32, *after)
            V["m"] = ran
        elif op == "n":
            gain_second, grad_middle, send_own = norm_back_block(
                1, middle, V["m"], tie(V["S"], *after), cot, gains, (F32, BF16)
            )
            send_mix = (send_own, link_x.swap(send_own, "x"))
            ran = send_own
        elif op == "o":
            ran = ffn_sum(2 * dv, dv, 1, BF16, *after)
            V["q"] = ran
        elif op == "Q":
            name = "ASqI"[j]
            V[name] = link_x.swap(V[name], "x")
        elif op == "w":
            ran = ffn_sum(2 * dv, dv, 0, F32, *after)
            V["w"] = ran
        elif op == "X":
            out_own = add(middle, V["w"], V["q"])
            V["X"] = give_back_x(out_own)
        elif op in "ZG":
            if op + "0" not in V:
                V[op + "0"] = spread_blocks(at, *((out_own, V["X"]) if op == "Z" else (grad_stream, V["K"])))
            shifts = ((2,), (1, 3), (1, 2, 3))[j]
            sends = [(V[op + "0"][k], XCZ, turned_pairs(round_pairs(k))) for k in shifts]
            for k, result in zip(shifts, link_z.group(sends)):
                V[op, k] = result
        elif op == "t":
            fs.turn(j)
        elif op == "c":
            fs.cross(j)
        elif op == "p":
            fs.pass_on(j)
        elif op == "T":
            ms.turn(j)
        elif op == "C":
            ms.cross(j)
        elif op == "P":
            ms.pass_on(j)
        elif op == "a":
            token_grads[j] = mix_back_block(
                tie(spots[j], *after), send_mix, mix_rows[j], kept[j][:4], dk, dv
            )
            ran = token_grads[j]
        elif op == "b":
            mix_grads[j] = mix_grad_block(send_mix, normed_in, merged[j], tie(token_grads[j], *after))
            ran = mix_grads[j][3]
        elif op == "i":
            ran = sum_blocks([tie(token_grads[0], *after)] + token_grads[1:], mix_rows, 0, dv, count, 1, BF16)
            V["I"] = ran
        elif op == "j":
            ran = sum_blocks([tie(token_grads[0], *after)] + token_grads[1:], mix_rows, 0, dv, count, 0, F32)
            V["j"] = ran
        elif op == "k":
            gain_first, grad_stream = norm_back_block(
                0, own_stream, V["j"], tie(V["I"], *after), grad_middle, gains, (BF16,)
            )
            V["K"] = give_back_x(grad_stream)
            ran = grad_stream
        elif op == "F":
            assert not fs.steps
            ffn_end = final_swap(fs.running)
        elif op == "M":
            assert not ms.steps
            mix_end = final_swap(tie(ms.running, V["G0"][0], V["E"]))
        elif op == "E":
            if j == 0:
                V["E"] = gain_totals(gain_first, gain_second)
            else:
                mine = gain_end(V["E"])
        else:
            raise ValueError(step)
        if ran is not None:
            last = [ran]
            fence.now.append(ran)
    out_blocks, grad_blocks = ([V[op + "0"][0], V[op, 1], V[op, 2], V[op, 3]] for op in "ZG")
    output = finish_tokens(at, out_blocks, BF16)

    grad_act, grad_lin, grad_down = finish_rows(
        at, *ffn_end, ((0, dv), (dv, dv), (2 * dv, dv)), (False,) * 3
    )
    grad_out, grad_gate, grad_value, grad_query, grad_key = finish_rows(
        at,
        *mix_end,
        ((0, dv), (dv, dv), (2 * dv, dv), (3 * dv, dk), (3 * dv + dk, dk)),
        (False, False, False, True, True),
    )
    grad_input = finish_tokens(tie(at, grad_act, grad_out, output, mine), grad_blocks, F32)
    return (
        output[:, None],
        grad_input[:, None],
        grad_query[None],
        grad_key[None],
        grad_value.T[None],
        grad_gate.T[None],
        grad_out[None],
        grad_act.T[None],
        grad_lin.T[None],
        grad_down[None],
        mine[:1],
        mine[1:],
    )


def placed(step, mesh, dp, tensor):
    tokens, columns = P(None, dp, tensor, None), P(None, dp, tensor)
    rows, gain = P(None, tensor, dp), P(None, dp)
    weights = (columns,) * 4 + (rows,) + (columns,) * 2 + (rows,)
    return jax.shard_map(
        step,
        mesh=mesh,
        in_specs=(tokens,) + weights + (gain, gain, tokens),
        out_specs=(tokens, tokens) + weights + (gain, gain),
        check_vma=False,
    )


def solution(mesh):
    if mesh.shape["dp"] == 8 and mesh.shape["tensor"] == 4:
        fine = jax.sharding.Mesh(mesh.devices.reshape(2, 2, 2, 4), ("y", "x", "c", "z"))
        return placed(paired, fine, ("y", "x", "c"), "z")
    return placed(shards, mesh, "dp", "tensor")
```

```python
import functools
import jax
import jax.numpy as jnp
from jax import lax
from jax.experimental import pallas as pl
from jax.experimental.pallas import tpu as pltpu
from jax.sharding import PartitionSpec as P

DK = 256
SEQ = 1024


eps_norm = 1e-06
group_eps = 1.0


def decay_table(head_count, first_head, length, key_size):
    head_ids = (first_head + jnp.arange(head_count, dtype=jnp.int32)).astype(jnp.float32)
    log_rates = jnp.log(1.0 - jnp.exp2(-5.0 - head_ids))
    positions = jnp.arange(length, dtype=jnp.int32)
    offsets = (positions[:, None] - positions[None, :]).astype(jnp.float32)
    causal = offsets >= 0.0
    powers = jnp.exp(jnp.where(causal, offsets, 0.0)[None] * log_rates[:, None, None])
    return jnp.where(causal[None], powers, 0.0) * key_size ** (-0.5)


def rms_inverse(stream, eps_value):
    return lax.rsqrt(jnp.mean(stream * stream, axis=-1, keepdims=True) + eps_value)


def spread_rows(normed_rows):
    return lax.all_gather(normed_rows, "tensor", axis=1, tiled=True)


def collect_rows(partial_value):
    return lax.psum_scatter(
        partial_value.astype(jnp.bfloat16), "tensor", scatter_dimension=1, tiled=True
    ).astype(jnp.float32)


def spread_grads(grad_rows):
    return lax.all_gather(grad_rows, "tensor", axis=1, tiled=True)


def collect_grads(partial_value):
    return lax.psum_scatter(
        partial_value.astype(jnp.bfloat16), "tensor", scatter_dimension=1, tiled=True
    ).astype(jnp.float32)


def fetch_layer(weight_set, layer_id):
    return (
        lax.all_gather(weight_set[0][layer_id], "dp", axis=0, tiled=True),
        lax.all_gather(weight_set[1][layer_id], "dp", axis=0, tiled=True),
        lax.all_gather(weight_set[2][layer_id], "dp", axis=0, tiled=True),
        lax.all_gather(weight_set[3][layer_id], "dp", axis=0, tiled=True),
        lax.all_gather(weight_set[4][layer_id], "dp", axis=1, tiled=True),
        lax.all_gather(weight_set[5][layer_id], "dp", axis=0, tiled=True),
        lax.all_gather(weight_set[6][layer_id], "dp", axis=0, tiled=True),
        lax.all_gather(weight_set[7][layer_id], "dp", axis=1, tiled=True),
        lax.all_gather(weight_set[8][layer_id], "dp", axis=0, tiled=True),
        lax.all_gather(weight_set[9][layer_id], "dp", axis=0, tiled=True),
    )


def project(in_rows, weight_mat):
    return jnp.einsum("bsd,de->bse", in_rows, weight_mat, preferred_element_type=jnp.float32)


def project_back(grad_rows, weight_mat):
    return jnp.einsum("bse,de->bsd", grad_rows, weight_mat, preferred_element_type=jnp.float32)


def weight_grad(in_rows, grad_rows):
    return jnp.einsum("bsd,bse->de", in_rows, grad_rows, preferred_element_type=jnp.float32)


def mix_forward(normed_in, layer_w, decays):
    batch_here = normed_in.shape[0]
    length = normed_in.shape[1]
    heads_here = decays.shape[0]
    queries = (
        project(normed_in, layer_w[0])
        .astype(jnp.bfloat16)
        .reshape(batch_here, length, heads_here, -1)
    )
    key_rows = (
        project(normed_in, layer_w[1])
        .astype(jnp.bfloat16)
        .reshape(batch_here, length, heads_here, -1)
    )
    values = (
        project(normed_in, layer_w[2])
        .astype(jnp.bfloat16)
        .reshape(batch_here, length, heads_here, -1)
    )
    gate_pre = project(normed_in, layer_w[3]).reshape(batch_here, length, heads_here, -1)
    scores = jnp.einsum("bnhk,bmhk->bhnm", queries, key_rows, preferred_element_type=jnp.float32)
    weights_mix = (scores * decays[None]).astype(jnp.bfloat16)
    retained = jnp.einsum(
        "bhnm,bmhv->bnhv", weights_mix, values, preferred_element_type=jnp.float32
    )
    inv_scale = rms_inverse(retained, group_eps)
    normed = retained * inv_scale
    merged = (jax.nn.silu(gate_pre) * normed).astype(jnp.bfloat16).reshape(batch_here, length, -1)
    partial_value = project(merged, layer_w[4])
    return (
        partial_value,
        (queries, key_rows, values, gate_pre, weights_mix, inv_scale, normed, merged),
    )


def mix_backward(normed_in, layer_w, decays, kept, grad_rows):
    queries, key_rows, values, gate_pre, weights_mix, inv_scale, normed, merged = kept
    batch_here = normed_in.shape[0]
    length = normed_in.shape[1]
    grad_w_out = weight_grad(merged, grad_rows)
    merged_grad = jnp.einsum(
        "bsd,ed->bse", grad_rows, layer_w[4], preferred_element_type=jnp.float32
    ).reshape(normed.shape)
    swish, swish_back = jax.vjp(jax.nn.silu, gate_pre)
    gate_grad = (
        swish_back(merged_grad * normed)[0].astype(jnp.bfloat16).reshape(batch_here, length, -1)
    )
    normed_grad = merged_grad * swish
    retained_grad = (
        inv_scale * (normed_grad - normed * jnp.mean(normed_grad * normed, axis=-1, keepdims=True))
    ).astype(jnp.bfloat16)
    mix_grad = jnp.einsum(
        "bnhv,bmhv->bhnm", retained_grad, values, preferred_element_type=jnp.float32
    )
    values_grad = (
        jnp.einsum(
            "bhnm,bnhv->bmhv", weights_mix, retained_grad, preferred_element_type=jnp.float32
        )
        .astype(jnp.bfloat16)
        .reshape(batch_here, length, -1)
    )
    score_grad = (mix_grad * decays[None]).astype(jnp.bfloat16)
    queries_grad = (
        jnp.einsum("bhnm,bmhk->bnhk", score_grad, key_rows, preferred_element_type=jnp.float32)
        .astype(jnp.bfloat16)
        .reshape(batch_here, length, -1)
    )
    keys_grad = (
        jnp.einsum("bhnm,bnhk->bmhk", score_grad, queries, preferred_element_type=jnp.float32)
        .astype(jnp.bfloat16)
        .reshape(batch_here, length, -1)
    )
    grads = (
        weight_grad(normed_in, queries_grad),
        weight_grad(normed_in, keys_grad),
        weight_grad(normed_in, values_grad),
        weight_grad(normed_in, gate_grad),
        grad_w_out,
    )
    in_grad = project_back(queries_grad, layer_w[0]) + project_back(keys_grad, layer_w[1])
    in_grad = in_grad + project_back(values_grad, layer_w[2]) + project_back(gate_grad, layer_w[3])
    return (in_grad, grads)


def ffn_forward(normed_mid, layer_w):
    act_pre = project(normed_mid, layer_w[5])
    lin_pre = project(normed_mid, layer_w[6])
    hidden = (jax.nn.gelu(act_pre) * lin_pre).astype(jnp.bfloat16)
    return (project(hidden, layer_w[7]), (act_pre, lin_pre, hidden))


def ffn_backward(normed_mid, layer_w, kept, grad_rows):
    act_pre, lin_pre, hidden = kept
    grad_w_down = weight_grad(hidden, grad_rows)
    grad_hidden = jnp.einsum(
        "bsd,fd->bsf", grad_rows, layer_w[7], preferred_element_type=jnp.float32
    )
    gelu_val, gelu_back = jax.vjp(jax.nn.gelu, act_pre)
    act_grad = gelu_back(grad_hidden * lin_pre)[0].astype(jnp.bfloat16)
    lin_grad = (grad_hidden * gelu_val).astype(jnp.bfloat16)
    in_grad = project_back(act_grad, layer_w[5]) + project_back(lin_grad, layer_w[6])
    return (
        in_grad,
        (weight_grad(normed_mid, act_grad), weight_grad(normed_mid, lin_grad), grad_w_down),
    )


def norm_forward(stream, gain_row):
    return (stream * rms_inverse(stream, eps_norm) * gain_row).astype(jnp.bfloat16)


def norm_backward(stream, gain_row, grad_norm):
    inv_scale = rms_inverse(stream, eps_norm)
    unit_rows = stream * inv_scale
    grad_gain = jnp.sum(grad_norm * unit_rows, axis=(0, 1))
    grad_unit = grad_norm * gain_row
    grad_stream = inv_scale * (
        grad_unit - unit_rows * jnp.mean(grad_unit * unit_rows, axis=-1, keepdims=True)
    )
    return (grad_stream, grad_gain)


def shards(
    inputs,
    w_query,
    w_key,
    w_value,
    w_gate,
    w_out,
    w_act,
    w_lin,
    w_down,
    gain_mix,
    gain_ffn,
    cotangent,
):
    weight_set = (w_query, w_key, w_value, w_gate, w_out, w_act, w_lin, w_down, gain_mix, gain_ffn)
    layer_count = w_query.shape[0]
    micro_count = inputs.shape[0]
    heads_here = w_query.shape[2] // DK
    decays = decay_table(heads_here, lax.axis_index("tensor") * heads_here, SEQ, DK)
    streams = [inputs[micro_id].astype(jnp.float32) for micro_id in range(micro_count)]
    layer_id = 0
    layer_records = []
    for micro_id in range(micro_count):
        current = fetch_layer(weight_set, layer_id)
        stream = streams[micro_id]
        normed_in = spread_rows(norm_forward(stream, current[8].astype(jnp.float32)))
        partial_value, mix_kept = mix_forward(normed_in, current, decays)
        middle = stream + collect_rows(partial_value)
        normed_mid = spread_rows(norm_forward(middle, current[9].astype(jnp.float32)))
        partial_value, ffn_kept = ffn_forward(normed_mid, current)
        streams[micro_id] = middle + collect_rows(partial_value)
        layer_records.append((stream, normed_in, mix_kept, middle, normed_mid, ffn_kept))
    records = [layer_records]
    grads_now = [cotangent[micro_id].astype(jnp.float32) for micro_id in range(micro_count)]
    layer_sums = [None] * layer_count
    for layer_id in reversed(range(layer_count)):
        for micro_id in range(micro_count):
            current = fetch_layer(weight_set, layer_id)
            stream, normed_in, mix_kept, middle, normed_mid, ffn_kept = records[layer_id][micro_id]
            grad_stream = grads_now[micro_id]
            grad_rows = spread_grads(grad_stream.astype(jnp.bfloat16))
            in_grad, ffn_grads = ffn_backward(normed_mid, current, ffn_kept, grad_rows)
            grad_mid, gain_second = norm_backward(
                middle, current[9].astype(jnp.float32), collect_grads(in_grad)
            )
            grad_middle = grad_stream + grad_mid
            grad_rows = spread_grads(grad_middle.astype(jnp.bfloat16))
            in_grad, mix_grads = mix_backward(normed_in, current, decays, mix_kept, grad_rows)
            grad_first, gain_first = norm_backward(
                stream, current[8].astype(jnp.float32), collect_grads(in_grad)
            )
            grads_now[micro_id] = grad_middle + grad_first
            terms = mix_grads + ffn_grads + (gain_first, gain_second)
            if micro_id == 0:
                layer_sums[layer_id] = terms
            else:
                layer_sums[layer_id] = jax.tree.map(jnp.add, layer_sums[layer_id], terms)
    stacked = [jnp.stack([layer_sums[0][kind_id]]) for kind_id in range(10)]
    reduced = (
        lax.psum_scatter(
            stacked[0].astype(jnp.bfloat16), "dp", scatter_dimension=1, tiled=True
        ).astype(jnp.float32),
        lax.psum_scatter(
            stacked[1].astype(jnp.bfloat16), "dp", scatter_dimension=1, tiled=True
        ).astype(jnp.float32),
        lax.psum_scatter(
            stacked[2].astype(jnp.bfloat16), "dp", scatter_dimension=1, tiled=True
        ).astype(jnp.float32),
        lax.psum_scatter(
            stacked[3].astype(jnp.bfloat16), "dp", scatter_dimension=1, tiled=True
        ).astype(jnp.float32),
        lax.psum_scatter(
            stacked[4].astype(jnp.bfloat16), "dp", scatter_dimension=2, tiled=True
        ).astype(jnp.float32),
        lax.psum_scatter(
            stacked[5].astype(jnp.bfloat16), "dp", scatter_dimension=1, tiled=True
        ).astype(jnp.float32),
        lax.psum_scatter(
            stacked[6].astype(jnp.bfloat16), "dp", scatter_dimension=1, tiled=True
        ).astype(jnp.float32),
        lax.psum_scatter(
            stacked[7].astype(jnp.bfloat16), "dp", scatter_dimension=2, tiled=True
        ).astype(jnp.float32),
        lax.psum_scatter(
            stacked[8].astype(jnp.bfloat16), "dp", scatter_dimension=1, tiled=True
        ).astype(jnp.float32),
        lax.psum_scatter(
            stacked[9].astype(jnp.bfloat16), "dp", scatter_dimension=1, tiled=True
        ).astype(jnp.float32),
    )
    gain_sums = lax.psum((reduced[8], reduced[9]), "tensor")
    output = jnp.stack(streams).astype(jnp.bfloat16)
    grad_input = jnp.stack(grads_now)
    return (
        output,
        grad_input,
        reduced[0],
        reduced[1],
        reduced[2],
        reduced[3],
        reduced[4],
        reduced[5],
        reduced[6],
        reduced[7],
        gain_sums[0],
        gain_sums[1],
    )


def cost(flops, bytes_accessed, transcendentals):
    return pl.CostEstimate(int(flops*0.3)+1, 0, int(bytes_accessed*0.3)+1)


F32, BF16 = jnp.float32, jnp.bfloat16


def dot_nt(a, b):
    return lax.dot_general(a, b, (((1,), (1,)), ((), ())), preferred_element_type=F32)


def dot_nn(a, b):
    return lax.dot_general(a, b, (((1,), (0,)), ((), ())), preferred_element_type=F32)


def dot_tn(a, b):
    return lax.dot_general(a, b, (((0,), (0,)), ((), ())), preferred_element_type=F32)


PARAMS = pltpu.CompilerParams(vmem_limit_bytes=48 * 1024 * 1024)
GELU_A = 0.7978845608028654
GELU_B = 0.044715
VM = pl.BlockSpec(memory_space=pltpu.VMEM)
SM = pl.BlockSpec(memory_space=pltpu.SMEM)
ANY = pl.BlockSpec(memory_space=pl.ANY)


def by_case(value, count, body):
    for case in range(count):

        @pl.when(value == case)
        def _(case=case):
            body(case)


def shape_of(shape, dtype):
    return jax.ShapeDtypeStruct(shape, dtype)


def weight_copies(pieces, first, last, held, sems):
    width = pieces[0].shape[1]
    return [
        pltpu.make_async_copy(
            piece.at[pl.ds(first, last - first)], held.at[:, pl.ds(p * width, width)], sems.at[p]
        )
        for p, piece in enumerate(pieces)
    ]


def ffn_kernel(dv, first, x_ref, c_ref, f0, f1, f2, f3, act_ref, held, sems):
    copies = weight_copies((f0, f1, f2, f3), 0, 3 * dv, held, sems)
    for copy in copies:
        copy.start()
    for copy in copies:
        copy.wait()
    act = dot_nt(held[:dv], x_ref[...])
    lin = dot_nt(held[dv : 2 * dv], x_ref[...])
    grad_hidden = dot_nt(held[2 * dv :], c_ref[first : first + x_ref.shape[0]])
    square = act * act
    tanh = jnp.tanh(GELU_A * (act + GELU_B * (square * act)))
    gelu = 0.5 * act * (1.0 + tanh)
    slope = 0.5 * (1.0 + tanh) + 0.5 * act * (1.0 - tanh * tanh) * (
        GELU_A * (1.0 + 3.0 * GELU_B * square)
    )
    act_ref[:dv] = (grad_hidden * lin * slope).astype(BF16)
    act_ref[dv : 2 * dv] = (grad_hidden * gelu).astype(BF16)
    act_ref[2 * dv :] = (gelu * lin).astype(BF16)


def ffn_block(x, cot, pieces, half):
    tokens, dv, width = x.shape[0], pieces[0].shape[0] // 3, pieces[0].shape[1]
    return pl.pallas_call(
        functools.partial(ffn_kernel, dv, half * tokens),
        out_shape=shape_of((3 * dv, tokens), BF16),
        in_specs=[VM, VM] + [ANY] * 4,
        out_specs=VM,
        scratch_shapes=[pltpu.VMEM((3 * dv, 4 * width), BF16), pltpu.SemaphoreType.DMA((4,))],
        compiler_params=PARAMS,
        cost_estimate=cost(
            flops=24 * tokens * dv * width, bytes_accessed=12 << 20, transcendentals=tokens * dv
        ),
        name="ffn_block",
    )(x, cot, *pieces)


def ffn_grad_kernel(dv, x0, x1, c_ref, a0, a1, *outs):
    side = outs[0].shape[1]
    half = x0.shape[0]
    for p, target in enumerate(outs):
        cols = slice(p * side, (p + 1) * side)
        for k in range(3):
            rows = slice(k * dv, (k + 1) * dv)
            parts = (c_ref[:half, cols], c_ref[half:, cols]) if k == 2 else (x0[:, cols], x1[:, cols])
            target[rows] = (dot_nn(a0[rows], parts[0]) + dot_nn(a1[rows], parts[1])).astype(BF16)


def ffn_grad_block(xs, cot, acts):
    rows, side = acts[0].shape[0], cot.shape[1] // 4
    grads = shape_of((rows, side), BF16)
    return pl.pallas_call(
        functools.partial(ffn_grad_kernel, rows // 3),
        out_shape=(grads,) * 4,
        in_specs=[VM] * 5,
        out_specs=(VM,) * 4,
        compiler_params=PARAMS,
        cost_estimate=cost(
            flops=8 * cot.shape[0] * rows * side, bytes_accessed=16 << 20, transcendentals=0
        ),
        name="ffn_grad_block",
    )(*xs, cot, *acts)


def decays(rate, keys, queries):
    down = jnp.exp(-keys.astype(F32) * rate) * 0.0625
    up = jnp.exp(queries.astype(F32) * rate)
    return jnp.where(queries >= keys, down * up, 0.0)


def log_rate(spots_ref):
    return jnp.log(1.0 - jnp.exp2(jnp.full((1, 1), -5.0, F32) - spots_ref[0].astype(F32)))


def tiles_of(x, length):
    half = length // 2
    early = slice(x * half, (x + 1) * half)
    late = slice((1 - x) * half, (2 - x) * half)
    lanes = lax.broadcasted_iota(jnp.int32, (1, half), 1)
    below = lax.broadcasted_iota(jnp.int32, (half, 1), 0)
    every = lax.broadcasted_iota(jnp.int32, (length, 1), 0)
    every = lax.rem(every + x * half, length)
    return (
        (early, early, below, lanes),
        (slice(None), late, every, lanes + half),
    )


def mix_kernel(
    dk, dv, spots_ref, x_ref, m0, m1, m2, m3, vqk_ref, g_ref, nrm_ref, inv_ref, out_ref, held, sems
):
    copies = weight_copies((m0, m1, m2, m3), dv, 3 * dv + 2 * dk, held, sems)
    for copy in copies:
        copy.start()
    for copy in copies:
        copy.wait()
    length = x_ref.shape[0]
    tile = 512

    def step(i, carry):
        rows = pl.ds(pl.multiple_of(i * tile, tile), tile)
        g_ref[:, rows] = dot_nt(held[:dv], x_ref[rows])
        vqk_ref[:, rows] = dot_nt(held[dv:], x_ref[rows]).astype(BF16)
        return carry

    lax.fori_loop(0, length // tile, step, 0)
    rate = log_rate(spots_ref)

    def attend(x):
        for keys, queries, key_spots, query_spots in tiles_of(x, length):
            scores = dot_tn(vqk_ref[dv + dk :, keys], vqk_ref[dv : dv + dk, queries])
            weights = (scores * decays(rate, key_spots, query_spots)).astype(BF16)
            retained = dot_nn(vqk_ref[:dv, keys], weights)
            inv = lax.rsqrt(jnp.mean(retained * retained, axis=0, keepdims=True) + 1.0)
            nrm = retained * inv
            gate = g_ref[:, queries]
            nrm_ref[:, queries] = nrm
            inv_ref[:, queries] = inv
            out_ref[:, queries] = (gate / (1.0 + jnp.exp(-gate)) * nrm).astype(BF16)

    by_case(spots_ref[1], 2, attend)


def mix_block(spots, x, pieces, dk, dv):
    tokens, width = x.shape[0], pieces[0].shape[1]
    return pl.pallas_call(
        functools.partial(mix_kernel, dk, dv),
        out_shape=(
            shape_of((dv + 2 * dk, tokens), BF16),
            shape_of((dv, tokens), F32),
            shape_of((dv, tokens), F32),
            shape_of((1, tokens), F32),
            shape_of((dv, tokens), BF16),
        ),
        in_specs=[SM, VM] + [ANY] * 4,
        out_specs=(VM,) * 5,
        scratch_shapes=[
            pltpu.VMEM((2 * dv + 2 * dk, 4 * width), BF16),
            pltpu.SemaphoreType.DMA((4,)),
        ],
        compiler_params=PARAMS,
        cost_estimate=cost(
            flops=2 * tokens * (2 * dk + 2 * dv) * x.shape[1] + 2 * tokens * tokens * (dk + dv),
            bytes_accessed=17 << 20,
            transcendentals=tokens * dv,
        ),
        name="mix_block",
    )(spots, x, *pieces)


def mix_back_kernel(
    dk, dv, spots_ref, s0, s1, m0, m1, m2, m3, vqk_ref, g_ref, nrm_ref, inv_ref,
    grad_ref, held, dv_ref, dk_ref, rg_ref, sems
):
    copies = weight_copies((m0, m1, m2, m3), 0, dv, held, sems)
    for copy in copies:
        copy.start()
    for copy in copies:
        copy.wait()
    half = s0.shape[0]
    length = 2 * half
    q_rows, k_rows = slice(2 * dv, 2 * dv + dk), slice(2 * dv + dk, 2 * dv + 2 * dk)
    for i, s_ref in enumerate((s0, s1)):
        rows = slice(i * half, (i + 1) * half)
        merged_grad = dot_nt(held[...], s_ref[...])
        gate, nrm = g_ref[:, rows], nrm_ref[:, rows]
        sig = 1.0 / (1.0 + jnp.exp(-gate))
        grad_ref[:dv, rows] = (merged_grad * nrm * (sig * (1.0 + gate * (1.0 - sig)))).astype(BF16)
        normed_grad = merged_grad * (gate * sig)
        mean = jnp.mean(normed_grad * nrm, axis=0, keepdims=True)
        rg_ref[:, rows] = (inv_ref[:, rows] * (normed_grad - nrm * mean)).astype(BF16)
    rate = log_rate(spots_ref)
    def attend(x):
        early, late = tiles_of(x, length)
        for keys, queries, key_spots, query_spots in (late, early):
            decay = decays(rate, key_spots, query_spots)
            k_part, q_part = vqk_ref[dv + dk :, keys], vqk_ref[dv : dv + dk, queries]
            rg_part = rg_ref[:, queries]
            weights = (dot_tn(k_part, q_part) * decay).astype(BF16)
            score_grad = (dot_tn(vqk_ref[:dv, keys], rg_part) * decay).astype(BF16)
            grad_ref[q_rows, queries] = dot_nn(k_part, score_grad).astype(BF16)
            values_grad = dot_nt(rg_part, weights)
            keys_grad = dot_nt(q_part, score_grad)
            if keys == slice(None):
                dv_ref[...] = values_grad
                dk_ref[...] = keys_grad
            else:
                dv_ref[:, keys] += values_grad
                dk_ref[:, keys] += keys_grad

    by_case(spots_ref[1], 2, attend)
    grad_ref[dv : 2 * dv] = dv_ref[...].astype(BF16)
    grad_ref[k_rows] = dk_ref[...].astype(BF16)


def mix_back_block(spots, sides, pieces, kept, dk, dv):
    tokens, width = 2 * sides[0].shape[0], pieces[0].shape[1]
    return pl.pallas_call(
        functools.partial(mix_back_kernel, dk, dv),
        out_shape=shape_of((2 * dv + 2 * dk, tokens), BF16),
        in_specs=[SM, VM, VM] + [ANY] * 4 + [VM] * 4,
        out_specs=VM,
        scratch_shapes=[
            pltpu.VMEM((dv, 4 * width), BF16),
            pltpu.VMEM((dv, tokens), F32),
            pltpu.VMEM((dk, tokens), F32),
            pltpu.VMEM((dv, tokens), BF16),
            pltpu.SemaphoreType.DMA((4,)),
        ],
        compiler_params=PARAMS,
        cost_estimate=cost(
            flops=8 * tokens * dv * width + 2 * tokens * tokens * (2 * dv + 3 * dk),
            bytes_accessed=16 << 20,
            transcendentals=tokens * dv,
        ),
        name="mix_back_block",
    )(spots, *sides, *pieces, *kept)


def mix_grad_kernel(dv, s0, s1, x_ref, out_ref, grad_ref, *outs):
    side = outs[0].shape[1]
    count, half = grad_ref.shape[0], s0.shape[0]
    for p, target in enumerate(outs):
        cols = slice(p * side, (p + 1) * side)
        target[:dv] = (
            dot_nn(out_ref[:, :half], s0[:, cols]) + dot_nn(out_ref[:, half:], s1[:, cols])
        ).astype(BF16)
        for rows in (slice(0, dv), slice(dv, 2 * dv), slice(2 * dv, count)):
            target[dv + rows.start : dv + rows.stop] = dot_nn(
                grad_ref[rows], x_ref[:, cols]
            ).astype(BF16)


def mix_grad_block(sides, x, merged, grads):
    dv, side = merged.shape[0], x.shape[1] // 4
    rows = dv + grads.shape[0]
    out = shape_of((rows, side), BF16)
    return pl.pallas_call(
        functools.partial(mix_grad_kernel, dv),
        out_shape=(out,) * 4,
        in_specs=[VM] * 5,
        out_specs=(VM,) * 4,
        compiler_params=PARAMS,
        cost_estimate=cost(
            flops=8 * x.shape[0] * rows * side, bytes_accessed=20 << 20, transcendentals=0
        ),
        name="mix_grad_block",
    )(*sides, x, merged, grads)


def sum_kernel(n_blocks, source_first, first, count, lanes, *refs):
    sources, pieces = refs[:n_blocks], refs[n_blocks : 5 * n_blocks]
    out_ref, held_source, held, source_sems, sems = refs[5 * n_blocks :]
    width = held.shape[2]

    def into(j):
        return pl.ds(j * count, count)

    early = [
        pltpu.make_async_copy(
            sources[j].at[pl.ds(source_first, count), lanes], held_source.at[into(j)], source_sems.at[j]
        )
        for j in range(n_blocks)
    ]
    copies = [
        [
            pltpu.make_async_copy(
                pieces[4 * j + p].at[pl.ds(first, count)], held.at[p, into(j)], sems.at[p, j]
            )
            for j in range(n_blocks)
        ]
        for p in range(4)
    ]
    for copy in early + [copy for group in copies for copy in group]:
        copy.start()
    for copy in early:
        copy.wait()
    for p in range(4):
        for copy in copies[p]:
            copy.wait()
        out_ref[:, p * width : (p + 1) * width] = dot_tn(held_source[...], held[p]).astype(
            out_ref.dtype
        )


def sum_blocks(sources, blocks, source_first, first, count, half, out_type):
    tokens, width, n = sources[0].shape[1], blocks[0][0].shape[1], len(blocks)
    if half is None:
        half = 0
    else:
        tokens = tokens // 2
    return pl.pallas_call(
        functools.partial(
            sum_kernel, n, source_first, first, count, pl.ds(half * tokens, tokens)
        ),
        out_shape=shape_of((tokens, 4 * width), out_type),
        in_specs=[ANY] * (5 * n),
        out_specs=VM,
        scratch_shapes=[
            pltpu.VMEM((n * count, tokens), BF16),
            pltpu.VMEM((4, n * count, width), BF16),
            pltpu.SemaphoreType.DMA((n,)),
            pltpu.SemaphoreType.DMA((4, n)),
        ],
        compiler_params=PARAMS,
        cost_estimate=cost(
            flops=8 * tokens * count * n * width,
            bytes_accessed=8 * count * n * width + 2 * count * n * tokens + 16 * tokens * width,
            transcendentals=0,
        ),
        name="sum_blocks",
    )(*sources, *[piece for block in blocks for piece in block])


def piece_of(p, y, c):
    return 4 * ((p // 2 % 2) ^ y) + 2 * (p % 2) + ((p // 4) ^ c)


def spots_of(x, y, c, z):
    return jnp.stack([x, y, c, z]).astype(jnp.int32)


def split_kernel(at, local, *outs):
    z = at[3]
    width = local.shape[2] // 8

    def split(case):
        for k, out in enumerate(outs):
            micro = lax.rem(z - k + 4, 4) // 2
            for p in range(8):
                first = piece_of(p, case // 2, case % 2) * width
                out[:, p * width : (p + 1) * width] = local[micro, :, first : first + width]

    by_case(2 * at[1] + at[2], 4, split)


def split_blocks(at, local):
    block = shape_of(local.shape[1:], local.dtype)
    return pl.pallas_call(
        split_kernel,
        out_shape=(block,) * 4,
        in_specs=[SM, VM],
        out_specs=(VM,) * 4,
        compiler_params=PARAMS,
        cost_estimate=cost(flops=1196000000, bytes_accessed=3 * local.size * 2, transcendentals=0),
        name="split_blocks",
    )(at, local)


EPS = 1e-6


def assemble_kernel(normed, at, *refs):
    blocks, others = refs[:4], refs[4:8]
    x, c, z = at[0], at[2], at[3]
    here = ((z ^ c) & 1) == x
    count = blocks[0].shape[0]

    def put(sources):
        for k, source in enumerate(sources):
            spot = lax.rem(z + k - 2 * x + 4, 4)
            rows = pl.ds(pl.multiple_of(spot * count, count), count)
            if normed:
                gains, own, out = refs[8:]
                values = source[...].astype(F32)
                scale = lax.rsqrt(jnp.mean(values * values, axis=-1, keepdims=True) + EPS)
                out[rows] = (values * scale * gains[0:1]).astype(BF16)

                @pl.when(spot < 2)
                def _():
                    own[pl.ds(pl.multiple_of(lax.rem(spot, 2) * count, count), count)] = source[...]

            else:
                refs[8][rows] = source[...]

    @pl.when(here)
    def _():
        put(blocks)

    @pl.when(jnp.logical_not(here))
    def _():
        put(others)


def assemble(at, blocks, others, gains=None):
    count, width = blocks[0].shape
    whole, half = shape_of((4 * count, width), BF16), shape_of((2 * count, width), BF16)
    extra = [] if gains is None else [gains]
    return pl.pallas_call(
        functools.partial(assemble_kernel, gains is not None),
        out_shape=whole if gains is None else (half, whole),
        in_specs=[SM] + [VM] * (8 + len(extra)),
        out_specs=VM if gains is None else (VM, VM),
        compiler_params=PARAMS,
        cost_estimate=cost(
            flops=3380000000, bytes_accessed=24 * count * width, transcendentals=0
        ),
        name="assemble",
    )(at, *blocks, *others, *extra)


def middle_kernel(stream, partial, got, gains, middle, normed):
    tile = 128

    def step(i, carry):
        rows = pl.ds(pl.multiple_of(i * tile, tile), tile)
        values = stream[rows].astype(F32) + partial[rows] + got[rows].astype(F32)
        middle[rows] = values
        scale = lax.rsqrt(jnp.mean(values * values, axis=-1, keepdims=True) + EPS)
        normed[rows] = (values * scale * gains[1:2]).astype(BF16)
        return carry

    lax.fori_loop(0, stream.shape[0] // tile, step, 0)


def middle_block(stream, partial, got, gains):
    return pl.pallas_call(
        middle_kernel,
        out_shape=(shape_of(stream.shape, F32), shape_of(stream.shape, BF16)),
        in_specs=[VM] * 4,
        out_specs=(VM, VM),
        compiler_params=PARAMS,
        cost_estimate=cost(flops=3796000000, bytes_accessed=14 * stream.size, transcendentals=0),
        name="middle_block",
    )(stream, partial, got, gains)


def norm_back_kernel(row, base, partial, got, grad, gains, *outs):
    tile = 128
    total_ref = outs[0]
    total_ref[...] = jnp.zeros_like(total_ref)
    gain = gains[row : row + 1]

    def step(i, carry):
        rows = pl.ds(pl.multiple_of(i * tile, tile), tile)
        values = base[rows].astype(F32)
        grad_norm = partial[rows] + got[rows].astype(F32)
        scale = lax.rsqrt(jnp.mean(values * values, axis=-1, keepdims=True) + EPS)
        unit = values * scale
        total_ref[...] += jnp.sum(grad_norm * unit, axis=0, keepdims=True)
        inner = grad_norm * gain
        mean = jnp.mean(inner * unit, axis=-1, keepdims=True)
        result = grad[rows].astype(F32) + scale * (inner - unit * mean)
        for out in outs[1:]:
            out[rows] = result.astype(out.dtype)
        return carry

    lax.fori_loop(0, base.shape[0] // tile, step, 0)


def norm_back_block(row, base, partial, got, grad, gains, types):
    return pl.pallas_call(
        functools.partial(norm_back_kernel, row),
        out_shape=(shape_of((1, base.shape[1]), F32),)
        + tuple(shape_of(base.shape, kind) for kind in types),
        in_specs=[VM] * 5,
        out_specs=(VM,) * (1 + len(types)),
        compiler_params=PARAMS,
        cost_estimate=cost(flops=5200000000, bytes_accessed=20 * base.size, transcendentals=0),
        name="norm_back_block",
    )(base, partial, got, grad, gains)


def spread_kernel(at, own, *refs):
    x, z = at[0], at[3]
    count = refs[0].shape[0]
    for k, out in enumerate(refs[2:]):
        block = lax.rem(z + k, 4)
        rows = pl.ds(pl.multiple_of(lax.rem(block, 2) * count, count), count)

        @pl.when(block // 2 == x)
        def _(out=out, rows=rows):
            out[...] = own[rows]

        for part in range(2):

            @pl.when((block // 2 != x) & (lax.rem(block, 2) == part))
            def _(out=out, other=refs[part]):
                out[...] = other[...]


def spread_blocks(at, own, others):
    block = shape_of((own.shape[0] // 2, own.shape[1]), own.dtype)
    return pl.pallas_call(
        spread_kernel,
        out_shape=(block,) * 4,
        in_specs=[SM, VM, VM, VM],
        out_specs=(VM,) * 4,
        compiler_params=PARAMS,
        cost_estimate=cost(flops=1820000000, bytes_accessed=8 * own.size, transcendentals=0),
        name="spread_blocks",
    )(at, own, *others)


def finish_kernel(at, b0, b1, b2, b3, out):
    x, y, c, z = (at[i] for i in range(4))
    width = out.shape[2] // 8
    for micro in range(2):
        source = lax.rem(z - 2 * micro - (x ^ c) + 8, 4)
        for k, block in enumerate((b0, b1, b2, b3)):

            @pl.when(source == k)
            def _(block=block, micro=micro):
                def put(case):
                    for p in range(8):
                        first = piece_of(p, case // 2, case % 2) * width
                        out[micro, :, first : first + width] = block[
                            :, p * width : (p + 1) * width
                        ].astype(out.dtype)

                by_case(2 * y + c, 4, put)


def finish_tokens(at, blocks, kind):
    count, width = blocks[0].shape
    return pl.pallas_call(
        finish_kernel,
        out_shape=shape_of((2, count, width), kind),
        in_specs=[SM] + [VM] * 4,
        out_specs=VM,
        compiler_params=PARAMS,
        cost_estimate=cost(flops=1560000000, bytes_accessed=16 * count * width, transcendentals=0),
        name="finish_tokens",
    )(at, *blocks)


def rows_kernel(spans, turned, at, mine, got, *refs):
    outs, held = refs[: len(spans)], refs[len(spans)]

    def put(x):
        for out, (first, count), turn in zip(outs, spans, turned):
            target = held if turn else out
            rows = slice(first, first + count)
            target[x * count : (x + 1) * count] = mine[rows].astype(F32)
            target[(1 - x) * count : (2 - x) * count] = got[rows].astype(F32)
            if turn:
                out[...] = held[...].T

    by_case(at[0], 2, put)


def finish_rows(at, mine, got, spans, turned):
    width = mine.shape[1]
    shapes = [(2 * n, width) for _, n in spans]
    held = max([n for (_, n), turn in zip(spans, turned) if turn] + [8])
    return pl.pallas_call(
        functools.partial(rows_kernel, spans, turned),
        out_shape=tuple(
            shape_of(s[::-1] if turn else s, F32) for s, turn in zip(shapes, turned)
        ),
        in_specs=[SM, VM, VM],
        out_specs=(VM,) * len(spans),
        scratch_shapes=[pltpu.VMEM((2 * held, width), F32)],
        compiler_params=PARAMS,
        cost_estimate=cost(flops=1560000000, bytes_accessed=12 * mine.size, transcendentals=0),
        name="finish_rows",
    )(at, mine, got)


O = {'xd': 2, 'yd': 1, 'zd': 2, 'scale': 0.3, 'back': ['B1', 'h3', 'r1', 'u2', 'B2', '|', 'r0', 'x1', 'v1', 'H0', 'x3', 'u3', 'B3', 'A', '|', '|', 'Q0', 'x2', 'v2', 'H1', 'D', '|', 'v3', 'H2', 'L', 'U0', 'U1', 'W', 'e0', 'e1', 'H3', 'f1', 'U2', '|', 'f0', 'f2', 'U3', 'f3', 's', '|', 'Q1', 'e2', 'g1', 't1', 'e3', 'g2', 'm', '|', 't2', 'c1', 'p1', 'c2', 'p2', 'n', 'g3', 't3', 'g0', 't0', 'o', 'c3', '|', '|', 'Q2', 'w', 'p3', 'a1', 'b1', 'T1', 'X', 'c0', 'a2', 'p0', 'b2', 'T2', '|', 'C1', 'Z2', 'a3', 'a0', 'b3', 'T3', '|', 'C2', 'P1', 'P2', 'i', 'b0', 'T0', '|', 'C3', 'P3', 'Q3', 'j', 'k', 'C0', '|', '|', 'G2', 'E0', 'P0', 'M', 'F', 'E1']}


SWAP = ((0, 1), (1, 0))
RING = ((0, 1), (1, 2), (2, 3), (3, 0))
XCZ = ("x", "c", "z")
ORDER = (1, 2, 3, 0)


def prepare_kernel(dk, dv, x_ref, q, k, v, g, o, a, n, d, gains, m_own, m_send, f_own, f_send, turned):
    def put(x, source, own, send, first, count):
        own[first : first + count] = source[x * count : (x + 1) * count]
        send[first : first + count] = source[(1 - x) * count : (2 - x) * count]

    def put_all(x):
        put(x, o, m_own, m_send, 0, dv)
        put(x, g, m_own, m_send, dv, dv)
        put(x, v, m_own, m_send, 2 * dv, dv)
        for i, source in enumerate((q, k)):
            turned[...] = source[...].T
            put(x, turned, m_own, m_send, 3 * dv + i * dk, dk)
        put(x, a, f_own, f_send, 0, dv)
        put(x, n, f_own, f_send, dv, dv)
        put(x, d, f_own, f_send, 2 * dv, dv)

    by_case(x_ref[0], 2, put_all)
    m_own[3 * dv + 2 * dk :] = gains[...]
    m_send[3 * dv + 2 * dk :] = gains[...]


def prepare(at, weights, gains, dk, dv):
    width = gains.shape[1]
    mix = shape_of((3 * dv + 2 * dk + 16, width), BF16)
    ffn = shape_of((3 * dv, width), BF16)
    return pl.pallas_call(
        functools.partial(prepare_kernel, dk, dv),
        out_shape=(mix, mix, ffn, ffn),
        in_specs=[SM] + [VM] * 9,
        out_specs=(VM,) * 4,
        scratch_shapes=[pltpu.VMEM((2 * dk, width), BF16)],
        compiler_params=PARAMS,
        name="prepare",
    )(at, *weights, gains)


def join_kernel(at, own, got, out):
    width = own.shape[1]

    def put(x):
        out[:, x * width : (x + 1) * width] = own[...]
        out[:, (1 - x) * width : (2 - x) * width] = got[...]

    by_case(at[0], 2, put)


def join(at, own, got):
    return pl.pallas_call(
        join_kernel,
        out_shape=shape_of((own.shape[0], 2 * own.shape[1]), BF16),
        in_specs=[SM, VM, VM],
        out_specs=VM,
        compiler_params=PARAMS,
        name="join",
    )(at, own, got)


def tie(value, *others):
    return lax.optimization_barrier((value,) + others)[0]


class Fence:
    def __init__(self):
        self.before, self.now = (), []

    def close(self, *more):
        self.before, self.now = tuple(self.now) + more, []


class Link:
    def __init__(self, fence, depth=1):
        self.fence, self.depth, self.ended = fence, depth, []

    def group(self, sends, *after, fenced=True):
        wait = self.ended[-self.depth] if len(self.ended) >= self.depth else ()
        if fenced:
            wait = wait + self.fence.before
        results = []
        for array, axis, pairs in sends:
            if wait + after:
                array = tie(array, *wait, *after)
            results.append(lax.ppermute(array, axis, pairs))
        self.ended.append(tuple(results))
        if fenced:
            self.fence.now += results
        return results

    def send(self, array, axis, pairs, *after):
        return self.group([(array, axis, pairs)], *after)[0]

    def swap(self, array, axis, *after):
        return self.send(array, axis, SWAP, *after)


def add(*terms):
    total = terms[0].astype(F32)
    for term in terms[1:]:
        total = total + term.astype(F32)
    return total.astype(BF16)


def pick(pair, index):
    return jnp.where(index == 0, pair[0], pair[1])


def home_pairs():
    pairs = []
    for c in range(2):
        for z in range(4):
            home = (z ^ c) & 1
            pairs.append((home * 8 + c * 4 + z, (1 - home) * 8 + c * 4 + z))
    return pairs


def round_pairs(shift):
    pairs = []
    for x in range(2):
        for c in range(2):
            for z in range(4):
                if (z & 1) == (x ^ c):
                    pairs.append((x * 8 + c * 4 + (z + shift) % 4, x * 8 + c * 4 + z))
    return pairs


def turned_pairs(pairs):
    return [(b, a) for a, b in pairs]


def paired(
    inputs,
    w_query,
    w_key,
    w_value,
    w_gate,
    w_out,
    w_act,
    w_lin,
    w_down,
    gain_mix,
    gain_ffn,
    cotangent,
):
    y, x, c, z = (lax.axis_index(name) for name in ("y", "x", "c", "z"))
    at = spots_of(x, y, c, z)
    dk, dv = DK, w_value.shape[2] // 2
    fence = Fence()
    link_x, link_y, link_z = (Link(fence, O[k]) for k in ("xd", "yd", "zd"))
    gains_here = jnp.concatenate(
        [gain_mix, gain_ffn, jnp.zeros((14, gain_mix.shape[1]), gain_mix.dtype)]
    )
    weights = [w_query[0], w_key[0], w_value[0].T, w_gate[0].T, w_out[0]]
    weights += [w_act[0].T, w_lin[0].T, w_down[0]]
    mix_rows, ffn_rows, merged, kept = [None] * 4, [None] * 4, [None] * 4, [None] * 4

    def swap_cores(array):
        return lax.ppermute(array, "c", SWAP)

    def turn_pieces(j, rows, current, over_y):
        rows[j] = (current, over_y) + tuple(
            swap_cores(tie(piece, *fence.before)) for piece in (current, over_y)
        )

    def home_send(block):
        return link_x.send(block, XCZ, home_pairs())

    spots = [jnp.stack([2 * ((z - j) % 4) + x, x]).astype(jnp.int32) for j in range(4)]

    def mix_forward(j, *after):
        kept[j] = mix_block(tie(spots[j], *after, *fence.before), normed_in, mix_rows[j], dk, dv)
        merged[j] = kept[j][-1]
        return merged[j]

    seq_parts = split_blocks(at, inputs[:, 0])
    seq_1, seq_3 = link_z.group([(seq_parts[k], XCZ, round_pairs(k)) for k in (1, 3)])
    mix_own, mix_send, ffn_own, ffn_send = prepare(
        tie(at, seq_parts[0]), weights, gains_here, dk, dv
    )
    mix_start = join(at, mix_own, link_x.swap(mix_send, "x"))
    fence.close()
    first = tie(mix_start, *fence.before)
    over_y = link_y.swap(first, "y")
    mix_1 = link_z.send(first, "z", RING)
    ffn_start = join(at, ffn_own, link_x.swap(ffn_send, "x"))
    other_0 = home_send(seq_parts[0])
    fence.close()
    turn_pieces(0, mix_rows, first, over_y)
    over_y = link_y.swap(ffn_start, "y")
    seq_2 = link_z.send(seq_parts[2], XCZ, round_pairs(2))
    other_1 = home_send(seq_1)
    fence.close()
    cot_parts = split_blocks(tie(at, *fence.before), cotangent[:, 0])
    turn_pieces(0, ffn_rows, ffn_start, over_y)
    over_y = link_y.swap(mix_1, "y")
    mix_2 = link_z.send(mix_1, "z", RING)
    other_3, other_2 = home_send(seq_3), home_send(seq_2)
    gains = jnp.concatenate(
        [piece[3 * dv + 2 * dk :] for piece in mix_rows[0]], axis=1
    ).astype(F32)
    fence.close()
    turn_pieces(1, mix_rows, mix_1, over_y)
    over_y = link_y.swap(mix_2, "y")
    mix_3 = link_z.send(mix_2, "z", RING)
    cot_other = home_send(cot_parts[0])
    own_stream, normed_in = assemble(
        tie(at, *fence.before),
        (seq_parts[0], seq_1, seq_2, seq_3),
        (other_0, other_1, other_2, other_3),
        gains,
    )
    half = own_stream.shape[0]
    fence.now.append(mix_forward(0))
    fence.close()
    mix_blocks = {0: mix_start, 1: mix_1, 2: mix_2, 3: mix_3}
    ffn_blocks = {0: ffn_start}
    mix_over, ffn_over = {2: over_y}, {}
    cot_blocks, cot_others = {0: cot_parts[0]}, {0: cot_other}
    acts, ffn_grads = [[None] * 4, [None] * 4], [None] * 4

    def ffn_sum(first, count, which, kind, *after):
        sources = list(acts[which])
        if after:
            sources[0] = tie(sources[0], *after)
        return sum_blocks(sources, ffn_rows, first, first, count, None, kind)

    class Scatter:
        def __init__(self, blocks):
            self.blocks, self.got, self.ready, self.over, self.running = blocks, {}, {}, {}, None
            self.passed, self.steps = {}, list(ORDER)

        def turn(self, j):
            own_0, own_1, send_0, send_1 = self.blocks[j]
            self.ready[j] = add(own_1, swap_cores(send_1))
            self.got[j] = (own_0, swap_cores(send_0))

        def cross(self, j, *after):
            self.over[j] = link_y.swap(self.ready[j], "y", self.got[j][1], *after)

        def pass_on(self, j):
            assert self.steps.pop(0) == j
            terms = self.got[j] + (self.over[j],)
            if self.running is None:
                self.running = add(*terms)
            else:
                self.passed[j] = link_z.send(self.running, "z", RING)
                self.running = add(self.passed[j], *terms)

    fs = Scatter(ffn_grads)
    V = {}

    def give_back_x(own_half):
        parts = own_half.reshape(2, own_half.shape[0] // 2, -1)
        return link_x.group([(part, XCZ, turned_pairs(home_pairs())) for part in (parts[0], parts[1])])

    def final_swap(block):
        side = block.shape[1] // 2
        keep = pick((block[:, :side], block[:, side:]), x)
        send = pick((block[:, side:], block[:, :side]), x)
        return keep, link_x.swap(send, "x")

    def gain_totals(*sums):
        sums, width = jnp.concatenate(sums), gain_mix.shape[1]
        total = jnp.concatenate(
            [
                lax.dynamic_slice_in_dim(sums, width * lax.bitwise_xor(4 * c + 2 * y, p), width, axis=1)
                for p in (0, 4, 1, 5, 2, 6, 3, 7)
            ],
            axis=1,
        )
        for axis in ("c", "y", "x"):
            total = total + lax.ppermute(tie(total, *fence.before), axis, SWAP)
        fence.now.append(total)
        return total

    def gain_end(total):
        total, width = tie(total, *fence.before), gain_mix.shape[1]
        turned = [
            lax.ppermute(total, "z", [(i, (i + shift) % 4) for i in range(4)]) for shift in (1, 2, 3)
        ]
        fence.now += turned
        total = total + turned[0] + turned[1] + turned[2]
        return lax.dynamic_slice_in_dim(total, width * (4 * y + 2 * x + c), width, axis=1)

    count = 2 * dv + 2 * dk
    token_grads, mix_grads = [None] * 4, [None] * 4
    ms = Scatter(mix_grads)
    last = []
    for step in O["back"]:
        op, j = step[0], int(step[1:] or 0)
        after = tuple(last) + fence.before
        ran = None
        if op == "|":
            fence.close()
        elif op == "h":
            mix_over[j] = link_y.swap(mix_blocks[j], "y")
        elif op == "H":
            ffn_over[j] = link_y.swap(ffn_blocks[j], "y")
        elif op == "u":
            turn_pieces(j, mix_rows, mix_blocks[j], mix_over[j])
        elif op == "U":
            turn_pieces(j, ffn_rows, ffn_blocks[j], ffn_over[j])
        elif op == "v":
            ffn_blocks[j] = link_z.send(ffn_blocks[j - 1], "z", RING)
        elif op == "r":
            shifts = ((2,), (1, 3), (1, 2, 3))[j]
            sends = [(cot_parts[k], XCZ, round_pairs(k)) for k in shifts]
            cot_blocks.update(zip(shifts, link_z.group(sends)))
        elif op == "x":
            cot_others[j] = home_send(cot_blocks[j])
        elif op == "B":
            ran = mix_forward(j, *last)
        elif op == "A":
            ran = V["A"] = sum_blocks([tie(merged[0], *after)] + merged[1:], mix_rows, 0, 0, dv, 1, BF16)
        elif op == "D":
            ran = sum_blocks([tie(merged[0], *after)] + merged[1:], mix_rows, 0, 0, dv, 0, F32)
            V["D"] = ran
        elif op == "L":
            middle, mid_own = middle_block(own_stream, tie(V["D"], *after), V["A"], gains)
            ran = mid_own
            mid_sides = (mid_own, link_x.swap(mid_own, "x"))
        elif op == "W":
            order = range(4)
            cot = assemble(
                tie(at, *after), [cot_blocks[k] for k in order], [cot_others[k] for k in order]
            )
            ran = cot
        elif op in "ef":
            which = "ef".index(op)
            acts[which][j] = ffn_block(tie(mid_sides[which], *after), cot, ffn_rows[j], which)
            ran = acts[which][j]
        elif op == "s":
            ran = V["S"] = ffn_sum(0, 2 * dv, 1, BF16, *after)
        elif op == "g":
            ffn_grads[j] = ffn_grad_block(mid_sides, cot, (tie(acts[0][j], *after), acts[1][j]))
            ran = ffn_grads[j][3]
        elif op == "m":
            ran = ffn_sum(0, 2 * dv, 0, F32, *after)
            V["m"] = ran
        elif op == "n":
            gain_second, grad_middle, send_own = norm_back_block(
                1, middle, V["m"], tie(V["S"], *after), cot, gains, (F32, BF16)
            )
            send_mix = (send_own, link_x.swap(send_own, "x"))
            ran = send_own
        elif op == "o":
            ran = ffn_sum(2 * dv, dv, 1, BF16, *after)
            V["q"] = ran
        elif op == "Q":
            name = "ASqI"[j]
            V[name] = link_x.swap(V[name], "x")
        elif op == "w":
            ran = ffn_sum(2 * dv, dv, 0, F32, *after)
            V["w"] = ran
        elif op == "X":
            out_own = add(middle, V["w"], V["q"])
            V["X"] = give_back_x(out_own)
        elif op in "ZG":
            if op + "0" not in V:
                V[op + "0"] = spread_blocks(at, *((out_own, V["X"]) if op == "Z" else (grad_stream, V["K"])))
            shifts = ((2,), (1, 3), (1, 2, 3))[j]
            sends = [(V[op + "0"][k], XCZ, turned_pairs(round_pairs(k))) for k in shifts]
            for k, result in zip(shifts, link_z.group(sends)):
                V[op, k] = result
        elif op == "t":
            fs.turn(j)
        elif op == "c":
            fs.cross(j)
        elif op == "p":
            fs.pass_on(j)
        elif op == "T":
            ms.turn(j)
        elif op == "C":
            ms.cross(j)
        elif op == "P":
            ms.pass_on(j)
        elif op == "a":
            token_grads[j] = mix_back_block(
                tie(spots[j], *after), send_mix, mix_rows[j], kept[j][:4], dk, dv
            )
            ran = token_grads[j]
        elif op == "b":
            mix_grads[j] = mix_grad_block(send_mix, normed_in, merged[j], tie(token_grads[j], *after))
            ran = mix_grads[j][3]
        elif op == "i":
            ran = sum_blocks([tie(token_grads[0], *after)] + token_grads[1:], mix_rows, 0, dv, count, 1, BF16)
            V["I"] = ran
        elif op == "j":
            ran = sum_blocks([tie(token_grads[0], *after)] + token_grads[1:], mix_rows, 0, dv, count, 0, F32)
            V["j"] = ran
        elif op == "k":
            gain_first, grad_stream = norm_back_block(
                0, own_stream, V["j"], tie(V["I"], *after), grad_middle, gains, (BF16,)
            )
            V["K"] = give_back_x(grad_stream)
            ran = grad_stream
        elif op == "F":
            assert not fs.steps
            ffn_end = final_swap(fs.running)
        elif op == "M":
            assert not ms.steps
            mix_end = final_swap(tie(ms.running, V["G0"][0], V["E"]))
        elif op == "E":
            if j == 0:
                V["E"] = gain_totals(gain_first, gain_second)
            else:
                mine = gain_end(V["E"])
        else:
            raise ValueError(step)
        if ran is not None:
            last = [ran]
            fence.now.append(ran)
    out_blocks, grad_blocks = ([V[op + "0"][0], V[op, 1], V[op, 2], V[op, 3]] for op in "ZG")
    output = finish_tokens(at, out_blocks, BF16)

    grad_act, grad_lin, grad_down = finish_rows(
        at, *ffn_end, ((0, dv), (dv, dv), (2 * dv, dv)), (False,) * 3
    )
    grad_out, grad_gate, grad_value, grad_query, grad_key = finish_rows(
        at,
        *mix_end,
        ((0, dv), (dv, dv), (2 * dv, dv), (3 * dv, dk), (3 * dv + dk, dk)),
        (False, False, False, True, True),
    )
    grad_input = finish_tokens(tie(at, grad_act, grad_out, output, mine), grad_blocks, F32)
    return (
        output[:, None],
        grad_input[:, None],
        grad_query[None],
        grad_key[None],
        grad_value.T[None],
        grad_gate.T[None],
        grad_out[None],
        grad_act.T[None],
        grad_lin.T[None],
        grad_down[None],
        mine[:1],
        mine[1:],
    )


def placed(step, mesh, dp, tensor):
    tokens, columns = P(None, dp, tensor, None), P(None, dp, tensor)
    rows, gain = P(None, tensor, dp), P(None, dp)
    weights = (columns,) * 4 + (rows,) + (columns,) * 2 + (rows,)
    return jax.shard_map(
        step,
        mesh=mesh,
        in_specs=(tokens,) + weights + (gain, gain, tokens),
        out_specs=(tokens, tokens) + weights + (gain, gain),
        check_vma=False,
    )


def solution(mesh):
    if mesh.shape["dp"] == 8 and mesh.shape["tensor"] == 4:
        fine = jax.sharding.Mesh(mesh.devices.reshape(2, 2, 2, 4), ("y", "x", "c", "z"))
        return placed(paired, fine, ("y", "x", "c"), "z")
    return placed(shards, mesh, "dp", "tensor")
```
